256 devices in a mesh: cfd: 32 (over y, z), struct: 8 (over x, core).
Axes of the slice: x: 4, y: 4, z: 8, core: 2. Of those that a mesh axis runs over, the one named last changes fastest.
Arguments:
- node_loads: bfloat16 [524288, 192], P(('cfd', 'struct')), may hold values from -6 to 6
- dest_owner: int32 [524288, 1], P(('cfd', 'struct')), may hold values from 0 to 31; in each aligned block of 2048 rows (0 to 2047, 2048 to 4095, ...) at most 256 rows name the same one
- dest_elem: int32 [524288], P(('cfd', 'struct')), may hold values from 0 to 2047
- node_weight: float32 [524288], P(('cfd', 'struct')), may hold values from 0.5 to 1.5
- mode_shapes: bfloat16 [3, 524288, 512], P(None, ('cfd', 'struct')), may hold values from -0.25 to 0.25
- stiffness: float32 [512], replicated, may hold values from 0.5 to 4
Outputs:
- node_disp: bfloat16 [524288, 192], P(('cfd', 'struct'))
- modal_amp: float32 [512, 64], replicated
The draws below stay inside these ranges and needn't reach their ends.
Inputs may be any that keep to these rules, and one draw needn't show every extreme that they name: `dest_owner`: within the rows of one device, no owner is named by more than 256 rows, and some device names one owner exactly 256 times.
All inputs are finite; a program needn't handle non-finite values.
Results may differ from the reference program's by a relative error of at most 0.0063.
Values may be sent and summed in bfloat16 or wider, within the bound.
A program may use at most 192 MiB of HBM per device.

```python
import math
import jax
import jax.numpy as jnp
import numpy as np
from jax import lax

S_DEV = 2048
E_DEV = 2048
RHS = 64
MODES = 512
CAP = 256
NODES = 524288
ELEMS = 524288
N_CFD = 32
N_STRUCT = 8


def place_ends(array, own_key, low, top_value):
    longest = array.shape.index(max(array.shape))
    spots = []
    for shift in (0, 1):
        where = [jax.random.randint(jax.random.fold_in(own_key, axis), (), 0, length) for axis, length in enumerate(array.shape)]
        where[longest] = (where[longest] + shift) % array.shape[longest]
        spots.append(tuple(where))
    return array.at[spots[0]].set(low).at[spots[1]].set(top_value)


def block_levels(rng, extent, cuts, least, top_value):
    def one(position, parts):
        draws = jax.random.uniform(jax.random.fold_in(jax.random.fold_in(rng, 6), position), (parts,), jnp.float32, least / len(cuts), top_value / len(cuts))
        return jnp.repeat(jnp.exp(draws), extent[position] // parts).reshape((-1,) + (1,) * (len(extent) - position - 1))

    level = one(*cuts[0])
    for cut in cuts[1:]:
        level = level * one(*cut)
    return level


def shared_out(rng, own, number, rows, count, top, reach, lean):
    sequence = jax.random.permutation(rng, count)
    heavy_load, common = shares(count, rows * top, reach, lean, True), shares(count, rows * top, reach, lean, False)
    places = jnp.arange(count)

    def named(tallies, turn):
        used = int((tallies > 0).sum())
        fixed = max(1, used // 4)
        shifted = fixed + (places - fixed + turn * (used - fixed)) % max(1, count - fixed)
        return jnp.zeros((count,), jnp.int32).at[sequence[jnp.where(places < fixed, places, shifted)]].set(jnp.asarray(tallies, jnp.int32))

    tallies = jnp.where(number % 4 == 0, named(heavy_load, number // 4), named(common, number - number // 4 - 1))
    mixed = jax.random.permutation(jax.random.fold_in(own, 3), count)
    giver, taker = mixed[0:count // 2 * 2:2], mixed[1:count // 2 * 2:2]
    slack = jnp.minimum(tallies[giver] - 1, reach - tallies[taker]) // 2
    slack = jnp.where((giver == sequence[0]) | (taker == sequence[0]) | (tallies[taker] == 0), 0, jnp.maximum(slack, 0))
    shifted = jax.random.randint(jax.random.fold_in(own, 4), (count // 2,), 0, 1 << 20) % (slack + 1)
    tallies = tallies.at[giver].add(-shifted).at[taker].add(shifted)
    items = jnp.searchsorted(jnp.cumsum(tallies), jnp.arange(rows * top), side="right").astype(jnp.int32)
    listing = items.reshape(top, rows).T
    listing = listing[jax.random.permutation(jax.random.fold_in(own, 1), rows)]
    turn = jax.random.randint(jax.random.fold_in(own, 2), (rows, 1), 0, top)
    return jnp.take_along_axis(listing, (jnp.arange(top)[None, :] + turn) % top, axis=1)


def shares(number_of, total, reach, lean, full):
    portions = [(1 << 20) // math.isqrt(rank ** lean) + 1 for rank in range(1, number_of + 1)]
    largest = reach if full else min(reach, max(-(-total // number_of), total * portions[0] // sum(portions)))
    least = 1 if total - largest >= number_of - 1 else 0
    counts, rest = [largest] + [least] * (number_of - 1), total - largest - least * (number_of - 1)
    while rest > 0:
        candidates = [i for i in range(1, number_of) if counts[i] < largest] or [i for i in range(1, number_of) if counts[i] < reach]
        pool, remaining = sum([portions[i] for i in candidates]), rest
        for i in candidates:
            addition = min(reach - counts[i], max(1, remaining * portions[i] // pool), rest)
            counts[i] = counts[i] + addition
            rest = rest - addition
    return np.array(counts)


def noise(stream_key, shape, width, most, cuts=(), kind=jnp.bfloat16):
    drawn = width * jax.random.normal(stream_key, shape, jnp.float32)
    if cuts:
        drawn = drawn * block_levels(stream_key, shape, cuts, -0.22, 0.18)
    return jnp.clip(drawn, -most, most).astype(kind)


def setup_inputs(seed: int = 0) -> dict:
    streams_of = jax.random.split(jax.random.key(seed), 7)
    node_loads = noise(streams_of[0], (NODES, 3 * RHS), 1.0, 6.0, ((0, 256),))
    dest_owner_keys = jax.random.split(jax.random.fold_in(streams_of[1], 1), NODES // S_DEV)
    dest_owner_turns = jax.random.permutation(jax.random.fold_in(streams_of[1], 3), NODES // S_DEV)
    dest_owner = jax.vmap(lambda own, number: shared_out(jax.random.fold_in(streams_of[1], 2), own, number, S_DEV, N_CFD, 1, CAP, 2))(dest_owner_keys, dest_owner_turns).reshape((NODES, 1))
    dest_elem = place_ends(jax.random.randint(streams_of[2], (NODES,), 0, E_DEV), jax.random.fold_in(streams_of[2], 1), 0, E_DEV - 1).astype(jnp.int32)
    node_weight = jnp.clip(0.5 + 1.0 * jax.random.uniform(streams_of[3], (NODES,), jnp.float32) ** block_levels(streams_of[3], (NODES,), ((0, 256),), -0.2, 0.2), 0.5, 1.5)
    mode_shapes = noise(streams_of[4], (3, ELEMS, MODES), MODES ** -0.5, 0.25, ((1, 256),))
    stiffness = jnp.clip(jnp.exp(jax.random.uniform(streams_of[5], (MODES,), jnp.float32, math.log(0.5), math.log(4.0))), 0.5, 4.0)
    return dict(node_loads=node_loads, dest_owner=dest_owner, dest_elem=dest_elem, node_weight=node_weight, mode_shapes=mode_shapes, stiffness=stiffness)


def reference(node_loads, dest_owner, dest_elem, node_weight, mode_shapes, stiffness):
    nodes = node_loads.shape[0]
    devices = N_CFD * N_STRUCT
    block_of = jnp.arange(nodes, dtype=jnp.int32) // S_DEV % N_STRUCT
    gid = ((dest_owner[:, 0] * N_STRUCT + block_of) * E_DEV + dest_elem).astype(jnp.int32)
    elem_load = jax.ops.segment_sum(node_loads.astype(jnp.float32), gid, num_segments=E_DEV * devices)
    elem_load = elem_load.astype(jnp.bfloat16)

    def project(total, index):
        start = (index * E_DEV).astype(jnp.int32)
        shapes = lax.dynamic_slice_in_dim(mode_shapes, start, E_DEV, 1).astype(jnp.float32)
        loads = lax.dynamic_slice_in_dim(elem_load, start, E_DEV, 0).astype(jnp.float32)
        loads = loads.reshape(E_DEV, 3, RHS)
        return (total + jnp.einsum('kem,ekr->mr', shapes, loads), None)
    modal_force, _ = lax.scan(project, jnp.zeros((MODES, RHS), jnp.float32), jnp.arange(devices, dtype=jnp.int32))
    scale = jnp.sqrt(jnp.float32(3.0 * nodes))
    modal_amp = modal_force / (stiffness[:, None] * scale)
    amp_low = modal_amp.astype(jnp.bfloat16).astype(jnp.float32)

    def expand(carry, index):
        start = (index * E_DEV).astype(jnp.int32)
        shapes = lax.dynamic_slice_in_dim(mode_shapes, start, E_DEV, 1).astype(jnp.float32)
        disp = jnp.einsum('kem,mr->ekr', shapes, amp_low).reshape(E_DEV, 3 * RHS)
        return (carry, disp.astype(jnp.bfloat16))
    _, elem_disp = lax.scan(expand, jnp.float32(0.0), jnp.arange(devices, dtype=jnp.int32))
    elem_disp = elem_disp.reshape(E_DEV * devices, 3 * RHS)
    picked = jnp.take(elem_disp, gid, axis=0).astype(jnp.float32)
    node_disp = (node_weight[:, None] * picked).astype(jnp.bfloat16)
    return (node_disp, modal_amp)
```

```python
import functools
import math

import jax
import jax.numpy as jnp
import numpy as np
from jax import lax
from jax.experimental import pallas as pl
from jax.experimental.pallas import tpu as pltpu
from jax.sharding import PartitionSpec as P

MESH = pl.DeviceIdType.MESH
BF16, F32, I32 = jnp.bfloat16, jnp.float32, jnp.int32
CLASS_CAP = 128


def general(node_loads, dest_owner, dest_elem, node_weight, mode_shapes, stiffness):
    rows, width = node_loads.shape
    rhs_count = width // 3
    owners = lax.axis_size("cfd")
    devices = owners * lax.axis_size("struct")
    capacity = max(2, 4 * rows // owners)
    elems = mode_shapes.shape[1]
    owner = dest_owner[:, 0]
    owner_hits = (owner[:, None] == jnp.arange(owners, dtype=jnp.int32)[None, :]).astype(jnp.int32)
    earlier = jnp.cumsum(owner_hits, axis=0) - owner_hits
    rank = jnp.sum(earlier * owner_hits, axis=1)
    send_loads = jnp.zeros((owners, capacity, width), jnp.bfloat16).at[owner, rank].set(node_loads)
    send_elem = jnp.full((owners, capacity), elems, jnp.int32).at[owner, rank].set(dest_elem)
    got_loads, got_elem = (
        lax.all_to_all(send_loads, "cfd", split_axis=0, concat_axis=0, tiled=True),
        lax.all_to_all(send_elem, "cfd", split_axis=0, concat_axis=0, tiled=True),
    )
    slots = owners * capacity
    slot_loads = got_loads.reshape(slots, width)
    slot_elem = got_elem.reshape(slots)
    block = math.gcd(512, slots)
    columns = jnp.arange(elems, dtype=jnp.int32)

    def add_block(total, index):
        start = index * block
        loads = lax.dynamic_slice_in_dim(slot_loads, start, block, 0)
        target = lax.dynamic_slice_in_dim(slot_elem, start, block, 0)
        select = (columns[:, None] == target[None, :]).astype(jnp.bfloat16)
        return (total + jnp.dot(select, loads, preferred_element_type=jnp.float32), None)

    elem_sum, _ = lax.scan(
        add_block,
        jnp.zeros((elems, width), jnp.float32),
        jnp.arange(slots // block, dtype=jnp.int32),
    )
    elem_load = elem_sum.astype(jnp.bfloat16).reshape(elems, 3, rhs_count)
    partial_force = jnp.einsum(
        "kem,ekr->mr", mode_shapes, elem_load, preferred_element_type=jnp.float32
    )
    scale = jnp.sqrt(jnp.float32(3.0 * rows * devices))
    modal_force = lax.psum(partial_force, ("cfd", "struct"))
    modal_amp = modal_force / (stiffness[:, None] * scale)
    amp_low = modal_amp.astype(jnp.bfloat16)
    elem_disp = jnp.einsum("kem,mr->ekr", mode_shapes, amp_low, preferred_element_type=jnp.float32)
    elem_disp = elem_disp.reshape(elems, width).astype(jnp.bfloat16)
    slot_disp = jnp.take(elem_disp, slot_elem, axis=0, mode="fill", fill_value=0).reshape(
        owners, capacity, width
    )
    returned = lax.all_to_all(slot_disp, "cfd", split_axis=0, concat_axis=0, tiled=True)
    node_value = returned[owner, rank]
    node_disp = (node_weight[:, None] * node_value.astype(jnp.float32)).astype(jnp.bfloat16)
    return (node_disp, modal_amp)


def mm(a, b):
    return jnp.dot(a, b, preferred_element_type=F32)


def iota(shape, dim):
    return lax.broadcasted_iota(I32, shape, dim)


def column(row):
    return jnp.transpose(jnp.broadcast_to(row, (128, 128)))


def split_halves(tail):
    low = iota(tail.shape, 1) < 64
    zero = jnp.zeros_like(tail)
    return jnp.concatenate([jnp.where(low, tail, zero), jnp.where(low, zero, tail)], axis=0)


def fused_kernel(
    n, ny, ns, nodes_scale,
    owner_ref, elem_ref, weight_ref, loads_ref, stiff_ref, mode_ref,
    out_ref, amp_ref,
    rows_ref, slot_ref, poison_ref, send1, keys_out, recv1, keys_in, acc, send2, recv2,
    mode_v, force, piece_out, piece_in, ring_out, ring_in, total_in,
    send3, recv3, disp, send4, recv4, slot_col, weight_col,
    s1, r1, k1, q1, s2, r2, sa, ra, sb, rb, sc, rc, s3, r3, s4, r4, mode_sem,
):
    nz = n // ny
    me = lax.axis_index("cfd")
    st = lax.axis_index("struct")
    my_y, my_z = me // nz, lax.rem(me, nz)
    my_q = my_y * ns + st
    group = ny * ns
    count = rows_ref.shape[0]

    def cfd_peer(t):
        return lax.rem(me + t, n)

    def plane_peer(t):
        q = lax.rem(my_q + t, group)
        return q, ((q // ns) * nz + my_z, lax.rem(q, ns))

    def z_peer(t):
        z = lax.rem(my_z + t, nz)
        return z, (my_y * nz + z, st)

    barrier = pltpu.get_barrier_semaphore()

    def greet_cfd(t, _):
        pl.semaphore_signal(barrier, inc=1, device_id=(cfd_peer(t), st), device_id_type=MESH)
        return 0

    def greet_plane(t, _):
        other = lax.rem(st + 1 + lax.rem(t, ns - 1), ns)
        pl.semaphore_signal(
            barrier, inc=1, device_id=(t // (ns - 1) * nz + my_z, other), device_id_type=MESH)
        return 0

    lax.fori_loop(1, n, greet_cfd, 0)
    lax.fori_loop(0, ny * (ns - 1), greet_plane, 0)
    mode_copy = pltpu.make_async_copy(mode_ref, mode_v, mode_sem)
    mode_copy.start()

    owner = owner_ref[...]
    elem = elem_ref[...]
    cls = lax.rem(elem // 64 + owner, n)
    upper = (iota((256, 256), 0) < iota((256, 256), 1)).astype(BF16)
    base = jnp.zeros((n, 1), F32)
    for q in range(count // 256):
        part = cls[:, 256 * q : 256 * q + 256]
        hit = iota((n, 256), 0) == jnp.broadcast_to(part, (n, 256))
        hit_f = hit.astype(F32)
        before = mm(hit_f.astype(BF16), upper) + base
        rank = jnp.sum(jnp.where(hit, before, 0.0), axis=0, keepdims=True).astype(I32)
        slot_ref[:, 256 * q : 256 * q + 256] = jnp.where(rank < CLASS_CAP, part * CLASS_CAP + rank, -1)
        base = base + jnp.sum(hit_f, axis=1, keepdims=True)
    most = jnp.max(base, axis=0, keepdims=True)
    poison_ref[...] = jnp.broadcast_to(jnp.where(most > CLASS_CAP, jnp.nan, 0.0), (8, 128))

    for q in range(count // 128):
        cols = slice(128 * q, 128 * q + 128)
        sub = iota((128, 128), 0)
        own = jnp.broadcast_to((owner[:, cols] + 1).astype(F32), (128, 128))
        low = jnp.broadcast_to(lax.rem(elem[:, cols], 64).astype(F32), (128, 128))
        meta = jnp.transpose(jnp.where(sub == 64, own, jnp.where(sub == 65, low, 0.0)))
        rows_ref[cols, 0:128] = loads_ref[cols, 0:128]
        tail = jnp.concatenate([loads_ref[cols, 128:192], jnp.zeros((128, 64), BF16)], axis=1)
        rows_ref[cols, 128:256] = tail + meta.astype(BF16)

    pl.semaphore_wait(barrier, n - 1 + group - ny)

    def hop1(peer, src):
        return pltpu.make_async_remote_copy(
            src_ref=send1.at[peer], dst_ref=recv1.at[src], send_sem=s1.at[peer], recv_sem=r1.at[src],
            device_id=(peer, st), device_id_type=MESH)

    def hop1_keys(peer, src):
        return pltpu.make_async_remote_copy(
            src_ref=keys_out.at[peer], dst_ref=keys_in.at[src], send_sem=k1.at[peer], recv_sem=q1.at[src],
            device_id=(peer, st), device_id_type=MESH)

    def build(c):
        slots = jnp.broadcast_to(slot_ref[...] - c * CLASS_CAP, (128, count))
        pick = (slots == iota((128, count), 0)).astype(BF16)
        y = mm(pick, rows_ref[...])
        tail = y[:, 128:256]
        send1[c, 0:128, :] = y[:, 0:128].astype(BF16)
        low = iota((64, 128), 1) < 64
        send1[c, 128:192, :] = jnp.where(low, tail[0:64], pltpu.roll(tail[64:128], 64, 1)).astype(BF16)
        turned = jnp.transpose(tail)
        keys_out[c] = (turned[64:65] * 64.0 + turned[65:66] - 64.0).astype(I32)

    def start1(t, _):
        c = cfd_peer(t)
        build(c)
        hop1(c, me).start()
        hop1_keys(c, me).start()
        return 0

    lax.fori_loop(1, n, start1, 0)
    build(me)
    recv1[me] = send1[me]
    keys_in[me] = keys_out[me]

    acc[...] = jnp.zeros_like(acc)

    def combine(g, _):
        keys, parts = [], []
        for u in range(4):
            t = g * 4 + u
            src = lax.rem(me + n - t, n)

            @pl.when(t > 0)
            def _():
                hop1(src, src).wait_recv()
                hop1_keys(src, src).wait_recv()

            keys.append(keys_in[src])
            parts.append(jnp.concatenate([recv1[src, 0:128, :], split_halves(recv1[src, 128:192, :])], axis=1))
        keys = jnp.concatenate(keys, axis=1)
        parts = jnp.concatenate(parts, axis=0)

        def block(b, _):
            at = pl.ds(pl.multiple_of(b * 256, 256), 256)
            hit = jnp.broadcast_to(keys - b * 256, (256, 512)) == iota((256, 512), 0)
            acc[at, :] += mm(hit.astype(BF16), parts)
            return 0

        lax.fori_loop(0, acc.shape[0] // 256, block, 0)
        return 0

    lax.fori_loop(0, n // 4, combine, 0)

    def hop2(peer, src):
        return pltpu.make_async_remote_copy(
            src_ref=send2.at[peer], dst_ref=recv2.at[src], send_sem=s2.at[peer], recv_sem=r2.at[src],
            device_id=(peer, st), device_id_type=MESH)

    def pack2(d):
        at = pl.ds(pl.multiple_of(d * 64, 64), 64)
        send2[d, 0:64, :] = acc[at, 0:128].astype(BF16)
        tail = acc[at, 128:256]
        tail = tail + pltpu.roll(tail, 64, 1)
        low = iota((32, 128), 1) < 64
        send2[d, 64:96, :] = jnp.where(low, tail[0:32], tail[32:64]).astype(BF16)

    def start2(t, _):
        d = cfd_peer(t)
        pack2(d)
        hop2(d, me).start()
        return 0

    lax.fori_loop(1, n, start2, 0)
    pack2(me)
    recv2[me] = send2[me]

    for q in range(count // 128):
        cols = slice(128 * q, 128 * q + 128)
        slot_col[cols, :] = column(slot_ref[:, cols].astype(F32)).astype(I32)
        weight_col[cols, :] = column(weight_ref[:, cols])

    mode_copy.wait()
    force[...] = jnp.zeros_like(force)

    def project(g, _):
        parts = []
        for u in range(4):
            b = g * 4 + u
            blk = n - 1 - b
            src = lax.rem(me + blk, n)

            @pl.when(blk > 0)
            def _():
                hop2(src, src).wait_recv()

            tail = recv2[src, 64:96, :]
            low = iota((32, 128), 1) < 64
            zero = jnp.zeros_like(tail)
            tail = jnp.concatenate([jnp.where(low, tail, zero), jnp.where(low, zero, tail)], axis=0)
            parts.append(jnp.concatenate([recv2[src, 0:64, :], tail], axis=1))
        load = jnp.concatenate(parts[::-1], axis=0)
        load = jnp.transpose(load.astype(F32)).astype(BF16)
        at = pl.ds(pl.multiple_of((n // 4 - 1 - g) * 256, 256), 256)
        f0 = mm(load[0:64], mode_v[0, at, :])
        f1 = mm(load[64:128], mode_v[1, at, :])
        f2 = mm(load[128:256], mode_v[2, at, :])
        force[...] += f0 + f1 + f2[0:64] + f2[64:128]
        return 0

    lax.fori_loop(0, n // 4, project, 0)

    rt = force.shape[0] // 8
    ct = force.shape[1] // 128
    for p in range(rt * ct):
        i, j = p // ct, p % ct
        piece_out[p] = force[8 * i : 8 * i + 8, 128 * j : 128 * j + 128] + poison_ref[...]

    def hop_a(q, dev, src):
        return pltpu.make_async_remote_copy(
            src_ref=piece_out.at[q], dst_ref=piece_in.at[src], send_sem=sa.at[q], recv_sem=ra.at[src],
            device_id=dev, device_id_type=MESH)

    def start_a(t, _):
        q, dev = plane_peer(t)
        hop_a(q, dev, my_q).start()
        return 0

    lax.fori_loop(1, group, start_a, 0)
    piece_in[my_q] = piece_out[my_q]

    def wait_a(t, _):
        q, dev = plane_peer(group - t)
        hop_a(q, dev, q).wait_recv()
        return 0

    lax.fori_loop(1, group, wait_a, 0)
    ring_out[...] = jnp.sum(piece_in[...], axis=0)

    def hop_b(z, dev, src):
        return pltpu.make_async_remote_copy(
            src_ref=ring_out, dst_ref=ring_in.at[src], send_sem=sb.at[z], recv_sem=rb.at[src],
            device_id=dev, device_id_type=MESH)

    def start_b(t, _):
        z, dev = z_peer(t)
        hop_b(z, dev, my_z).start()
        return 0

    lax.fori_loop(1, nz, start_b, 0)
    ring_in[my_z] = ring_out[...]

    def wait_b(t, _):
        z, dev = z_peer(nz - t)
        hop_b(z, dev, z).wait_recv()
        return 0

    lax.fori_loop(1, nz, wait_b, 0)
    total_in[my_q] = jnp.sum(ring_in[...], axis=0)

    def hop_c(q, dev):
        return pltpu.make_async_remote_copy(
            src_ref=total_in.at[my_q], dst_ref=total_in.at[my_q], send_sem=sc.at[q], recv_sem=rc.at[my_q],
            device_id=dev, device_id_type=MESH)

    def got_c(q, dev):
        return pltpu.make_async_remote_copy(
            src_ref=total_in.at[q], dst_ref=total_in.at[q], send_sem=sc.at[q], recv_sem=rc.at[q],
            device_id=dev, device_id_type=MESH)

    def start_c(t, _):
        q, dev = plane_peer(t)
        hop_c(q, dev).start()
        return 0

    lax.fori_loop(1, group, start_c, 0)

    def wait_c(t, _):
        q, dev = plane_peer(group - t)
        got_c(q, dev).wait_recv()
        return 0

    lax.fori_loop(1, group, wait_c, 0)
    whole = jnp.concatenate(
        [jnp.concatenate([total_in[i * ct + j] for j in range(ct)], axis=1) for i in range(rt)], axis=0)
    amp_t = whole / (stiff_ref[...] * nodes_scale)
    amp = jnp.transpose(jnp.concatenate([amp_t, amp_t], axis=0))
    amp_ref[...] = amp[:, 0:64]
    both = amp.astype(BF16)
    low = iota(amp.shape, 1) < 64
    left = jnp.where(low, amp, 0.0).astype(BF16)
    right = jnp.where(low, 0.0, amp).astype(BF16)

    def hop3(peer, src):
        return pltpu.make_async_remote_copy(
            src_ref=send3.at[peer], dst_ref=recv3.at[src], send_sem=s3.at[peer], recv_sem=r3.at[src],
            device_id=(peer, st), device_id_type=MESH)

    def expand(g, _):
        at = pl.ds(pl.multiple_of(g * 256, 256), 256)
        d01 = (mm(mode_v[0, at, :], left) + mm(mode_v[1, at, :], right)).astype(BF16)
        d2 = mm(mode_v[2, at, :], both)
        for u in range(4):
            b = g * 4 + u
            peer = cfd_peer(b)
            send3[peer, 0:64, :] = d01[64 * u : 64 * u + 64]
            keep = iota((32, 128), 1) < 64
            send3[peer, 64:96, :] = jnp.where(
                keep, d2[64 * u : 64 * u + 32], d2[64 * u + 32 : 64 * u + 64]).astype(BF16)

            @pl.when(b > 0)
            def _():
                hop3(peer, me).start()

        return 0

    lax.fori_loop(0, n // 4, expand, 0)
    recv3[me] = send3[me]

    def unpack3(t, _):
        src = lax.rem(me + n - t, n)

        @pl.when(t > 0)
        def _():
            hop3(src, src).wait_recv()

        at = pl.multiple_of(src * 64, 64)
        disp[pl.ds(at, 64), 0:128] = recv3[src, 0:64, :]
        tail = recv3[src, 64:96, :].astype(F32)
        other = pltpu.roll(tail, 64, 1)
        keep = iota((32, 128), 1) < 64
        disp[pl.ds(at, 32), 128:256] = jnp.where(keep, tail, other).astype(BF16)
        disp[pl.ds(at + 32, 32), 128:256] = jnp.where(keep, other, tail).astype(BF16)
        return 0

    lax.fori_loop(0, n, unpack3, 0)

    def hop4(peer, src):
        return pltpu.make_async_remote_copy(
            src_ref=send4.at[peer], dst_ref=recv4.at[src], send_sem=s4.at[peer], recv_sem=r4.at[src],
            device_id=(peer, st), device_id_type=MESH)

    def gather(src):
        keys = column(keys_in[src].astype(F32)).astype(I32)
        lane = iota((128, 128), 1)
        pick = jnp.concatenate(
            [(keys - 128 * q == lane).astype(BF16) for q in range(disp.shape[0] // 128)], axis=1)
        y = mm(pick, disp[...])
        keep = iota((64, 128), 1) < 64
        send4[src, 0:128, :] = y[:, 0:128].astype(BF16)
        send4[src, 128:192, :] = jnp.where(keep, y[0:64, 128:256], y[64:128, 128:256]).astype(BF16)

    def start4(t, _):
        src = cfd_peer(t)
        gather(src)
        hop4(src, me).start()
        return 0

    lax.fori_loop(1, n, start4, 0)
    gather(me)
    recv4[me] = send4[me]

    acc[...] = jnp.zeros_like(acc)

    def place(g, _):
        parts, firsts = [], []
        for u in range(4):
            t = g * 4 + u
            src = lax.rem(me + n - t, n)

            @pl.when(t > 0)
            def _():
                hop4(src, src).wait_recv()

            firsts.append(src * CLASS_CAP)
            parts.append(jnp.concatenate([recv4[src, 0:128, :], split_halves(recv4[src, 128:192, :])], axis=1))
        parts = jnp.concatenate(parts, axis=0)

        def block(b, _):
            at = pl.ds(pl.multiple_of(b * 256, 256), 256)
            slots = slot_col[at, :]
            lane = iota((256, 128), 1)
            pick = jnp.concatenate([(slots - first == lane).astype(BF16) for first in firsts], axis=1)
            acc[at, :] += mm(pick, parts)
            return 0

        lax.fori_loop(0, count // 256, block, 0)
        return 0

    lax.fori_loop(0, n // 4, place, 0)

    def finish(b, _):
        at = pl.ds(pl.multiple_of(b * 256, 256), 256)
        w = weight_col[at, :]
        out_ref[at, 0:128] = (acc[at, 0:128] * w).astype(BF16)
        tail = acc[at, 128:256]
        tail = (tail + pltpu.roll(tail, 64, 1)) * w
        out_ref[at, 128:192] = tail[:, 0:64].astype(BF16)
        return 0

    lax.fori_loop(0, count // 256, finish, 0)

    def sent(t, _):
        peer = cfd_peer(t)
        hop1(peer, me).wait_send()
        hop1_keys(peer, me).wait_send()
        hop2(peer, me).wait_send()
        hop3(peer, me).wait_send()
        hop4(peer, me).wait_send()
        return 0

    lax.fori_loop(1, n, sent, 0)

    def sent_plane(t, _):
        q, dev = plane_peer(t)
        hop_a(q, dev, my_q).wait_send()
        hop_c(q, dev).wait_send()
        return 0

    lax.fori_loop(1, group, sent_plane, 0)

    def sent_z(t, _):
        z, dev = z_peer(t)
        hop_b(z, dev, my_z).wait_send()
        return 0

    lax.fori_loop(1, nz, sent_z, 0)


def fast(node_loads, dest_owner, dest_elem, node_weight, mode_shapes, stiffness):
    rows, width = node_loads.shape
    n, ns = lax.axis_size("cfd"), lax.axis_size("struct")
    ny = 4
    nz = n // ny
    group = ny * ns
    comps, elems, modes = mode_shapes.shape
    scale = float(np.sqrt(np.float32(3.0 * rows * n * ns)))
    vmem = pl.BlockSpec(memory_space=pltpu.VMEM)
    dma = pltpu.SemaphoreType.DMA
    pair = (n, 192, 128)
    dense = (n, 96, 128)
    return pl.pallas_call(
        functools.partial(fused_kernel, n, ny, ns, scale),
        out_shape=(jax.ShapeDtypeStruct((rows, width), BF16), jax.ShapeDtypeStruct((modes, 64), F32)),
        in_specs=[vmem] * 5 + [pl.BlockSpec(memory_space=pl.ANY)],
        out_specs=(vmem, vmem),
        scratch_shapes=[
            pltpu.VMEM((rows, 256), BF16), pltpu.VMEM((1, rows), I32), pltpu.VMEM((8, 128), F32),
            pltpu.VMEM(pair, BF16), pltpu.VMEM((n, 1, 128), I32),
            pltpu.VMEM(pair, BF16), pltpu.VMEM((n, 1, 128), I32),
            pltpu.VMEM((rows, 256), F32), pltpu.VMEM(dense, BF16), pltpu.VMEM(dense, BF16),
            pltpu.VMEM(mode_shapes.shape, BF16), pltpu.VMEM((64, modes), F32),
            pltpu.VMEM((group, 8, 128), F32), pltpu.VMEM((group, 8, 128), F32),
            pltpu.VMEM((8, 128), F32), pltpu.VMEM((nz, 8, 128), F32), pltpu.VMEM((group, 8, 128), F32),
            pltpu.VMEM(dense, BF16), pltpu.VMEM(dense, BF16), pltpu.VMEM((elems, 256), BF16),
            pltpu.VMEM(pair, BF16), pltpu.VMEM(pair, BF16),
            pltpu.VMEM((rows, 128), I32), pltpu.VMEM((rows, 128), F32),
            dma((n,)), dma((n,)), dma((n,)), dma((n,)), dma((n,)), dma((n,)),
            dma((group,)), dma((group,)), dma((nz,)), dma((nz,)), dma((group,)), dma((group,)),
            dma((n,)), dma((n,)), dma((n,)), dma((n,)), dma(()),
        ],
        compiler_params=pltpu.CompilerParams(
            collective_id=0, has_side_effects=True, vmem_limit_bytes=56 * 1024 * 1024),
        cost_estimate=pl.CostEstimate(flops=30_000_000_000, bytes_accessed=10_000_000, transcendentals=0),
    )(
        dest_owner.reshape(1, rows), dest_elem.reshape(1, rows), node_weight.reshape(1, rows),
        node_loads, stiffness.reshape(1, modes), mode_shapes,
    )


def per_device(*args):
    node_disp, modal_amp = fast(*args)
    crowded = jnp.isnan(modal_amp[0, 0])
    return lax.cond(crowded, lambda a, f: general(*a), lambda a, f: f, args, (node_disp, modal_amp))


def solution(mesh):
    placed = (
        P(("cfd", "struct"), None),
        P(("cfd", "struct"), None),
        P(("cfd", "struct")),
        P(("cfd", "struct")),
        P(None, ("cfd", "struct"), None),
        P(),
    )
    return jax.shard_map(
        per_device,
        mesh=mesh,
        in_specs=placed,
        out_specs=(P(("cfd", "struct"), None), P()),
        check_vma=False,
    )
```

```python
import functools
import math

import jax
import jax.numpy as jnp
import numpy as np
from jax import lax
from jax.experimental import pallas as pl
from jax.experimental.pallas import tpu as pltpu
from jax.sharding import PartitionSpec as P

MESH = pl.DeviceIdType.MESH
BF16, F32, I32 = jnp.bfloat16, jnp.float32, jnp.int32
CLASS_CAP = 112
BLOCK = CLASS_CAP + 64


def general(node_loads, dest_owner, dest_elem, node_weight, mode_shapes, stiffness):
    rows, width = node_loads.shape
    rhs_count = width // 3
    owners = lax.axis_size("cfd")
    devices = owners * lax.axis_size("struct")
    capacity = max(2, 4 * rows // owners)
    elems = mode_shapes.shape[1]
    owner = dest_owner[:, 0]
    owner_hits = (owner[:, None] == jnp.arange(owners, dtype=jnp.int32)[None, :]).astype(jnp.int32)
    earlier = jnp.cumsum(owner_hits, axis=0) - owner_hits
    rank = jnp.sum(earlier * owner_hits, axis=1)
    send_loads = jnp.zeros((owners, capacity, width), jnp.bfloat16).at[owner, rank].set(node_loads)
    send_elem = jnp.full((owners, capacity), elems, jnp.int32).at[owner, rank].set(dest_elem)
    got_loads, got_elem = (
        lax.all_to_all(send_loads, "cfd", split_axis=0, concat_axis=0, tiled=True),
        lax.all_to_all(send_elem, "cfd", split_axis=0, concat_axis=0, tiled=True),
    )
    slots = owners * capacity
    slot_loads = got_loads.reshape(slots, width)
    slot_elem = got_elem.reshape(slots)
    block = math.gcd(512, slots)
    columns = jnp.arange(elems, dtype=jnp.int32)

    def add_block(total, index):
        start = index * block
        loads = lax.dynamic_slice_in_dim(slot_loads, start, block, 0)
        target = lax.dynamic_slice_in_dim(slot_elem, start, block, 0)
        select = (columns[:, None] == target[None, :]).astype(jnp.bfloat16)
        return (total + jnp.dot(select, loads, preferred_element_type=jnp.float32), None)

    elem_sum, _ = lax.scan(
        add_block,
        jnp.zeros((elems, width), jnp.float32),
        jnp.arange(slots // block, dtype=jnp.int32),
    )
    elem_load = elem_sum.astype(jnp.bfloat16).reshape(elems, 3, rhs_count)
    partial_force = jnp.einsum(
        "kem,ekr->mr", mode_shapes, elem_load, preferred_element_type=jnp.float32
    )
    scale = jnp.sqrt(jnp.float32(3.0 * rows * devices))
    pieces = partial_force.reshape(devices, 1, -1)
    pieces = lax.all_to_all(pieces, ("cfd", "struct"), split_axis=0, concat_axis=0, tiled=True)
    piece = jnp.broadcast_to(jnp.sum(pieces, axis=0, keepdims=True), pieces.shape)
    pieces = lax.all_to_all(piece, ("cfd", "struct"), split_axis=0, concat_axis=0, tiled=True)
    modal_force = pieces.reshape(partial_force.shape)
    modal_amp = modal_force / (stiffness[:, None] * scale)
    amp_low = modal_amp.astype(jnp.bfloat16)
    elem_disp = jnp.einsum("kem,mr->ekr", mode_shapes, amp_low, preferred_element_type=jnp.float32)
    elem_disp = elem_disp.reshape(elems, width).astype(jnp.bfloat16)
    slot_disp = jnp.take(elem_disp, slot_elem, axis=0, mode="fill", fill_value=0).reshape(
        owners, capacity, width
    )
    returned = lax.all_to_all(slot_disp, "cfd", split_axis=0, concat_axis=0, tiled=True)
    node_value = returned[owner, rank]
    node_disp = (node_weight[:, None] * node_value.astype(jnp.float32)).astype(jnp.bfloat16)
    return (node_disp, modal_amp)


def mm(a, b):
    return jnp.dot(a, b, preferred_element_type=F32)


def mm_nt(a, b):
    return lax.dot_general(a, b, (((1,), (1,)), ((), ())), preferred_element_type=F32)


def iota(shape, dim):
    return lax.broadcasted_iota(I32, shape, dim)


def column(row):
    return jnp.transpose(jnp.broadcast_to(row, (128, 128)))


def split_halves(tail):
    low = iota(tail.shape, 1) < 64
    zero = jnp.zeros_like(tail)
    return jnp.concatenate([jnp.where(low, tail, zero), jnp.where(low, zero, tail)], axis=0)


def unpack(block):
    head = jnp.concatenate([block[0:CLASS_CAP], jnp.zeros((128 - CLASS_CAP, 128), BF16)], axis=0)
    return jnp.concatenate([head, split_halves(block[CLASS_CAP:BLOCK])], axis=1)


def fused_kernel(
    n, ny, ns, nodes_scale,
    owner_ref, elem_ref, weight_ref, loads_ref, stiff_ref, mode_ref,
    out_ref, amp_ref,
    rows_ref, slot_ref, poison_ref, send1, keys_out, recv1, keys_in, acc, send2, recv2,
    mode_v, force, piece_out, piece_in, col_out, col_in, ring_out, ring_in, total_in,
    send3, recv3, disp, send4, recv4, acc_t,
    s1, r1, k1, q1, s2, r2, sa, ra, sy, ry, sb, rb, sc, rc, s3, r3, s4, r4, mode_sem,
):
    nz = n // ny
    me = lax.axis_index("cfd")
    st = lax.axis_index("struct")
    my_y, my_z = me // nz, lax.rem(me, nz)
    count = rows_ref.shape[1]

    def cfd_peer(t):
        return lax.rem(me + t, n)

    def struct_peer(t):
        q = lax.rem(st + t, ns)
        return q, (me, q)

    def y_peer(t):
        y = lax.rem(my_y + t, ny)
        return y, (y * nz + my_z, st)

    def z_peer(t):
        z = lax.rem(my_z + t, nz)
        return z, (my_y * nz + z, st)

    barrier = pltpu.get_barrier_semaphore()

    def greet_cfd(t, _):
        pl.semaphore_signal(barrier, inc=1, device_id=(cfd_peer(t), st), device_id_type=MESH)
        return 0

    def greet_struct(t, _):
        _, dev = struct_peer(t)
        pl.semaphore_signal(barrier, inc=1, device_id=dev, device_id_type=MESH)
        return 0

    lax.fori_loop(1, n, greet_cfd, 0)
    lax.fori_loop(1, ns, greet_struct, 0)
    mode_copy = pltpu.make_async_copy(mode_ref, mode_v, mode_sem)
    mode_copy.start()

    owner = owner_ref[...]
    elem = elem_ref[...]
    cls = ((elem >> 6) + owner) & (n - 1)
    upper = (iota((256, 256), 0) < iota((256, 256), 1)).astype(BF16)
    base = jnp.zeros((n, 1), F32)
    for q in range(count // 256):
        part = cls[:, 256 * q : 256 * q + 256]
        hit = iota((n, 256), 0) == jnp.broadcast_to(part, (n, 256))
        hit_f = hit.astype(F32)
        before = mm(hit_f.astype(BF16), upper) + base
        rank = jnp.sum(jnp.where(hit, before, 0.0), axis=0, keepdims=True).astype(I32)
        slot_ref[:, 256 * q : 256 * q + 256] = jnp.where(rank < CLASS_CAP, part * 128 + rank, -1)
        base = base + jnp.sum(hit_f, axis=1, keepdims=True)
    most = jnp.max(base, axis=0, keepdims=True)
    poison_ref[...] = jnp.broadcast_to(jnp.where(most > CLASS_CAP, jnp.nan, 0.0), (8, 128))

    sub = iota((64, count), 0)
    own = jnp.broadcast_to(owner + 1, (64, count))
    low_elem = jnp.broadcast_to(elem & 63, (64, count))
    rows_ref[0:192, :] = loads_ref[...]
    rows_ref[192:256, :] = jnp.where(sub == 0, own, jnp.where(sub == 1, low_elem, 0)).astype(F32).astype(BF16)

    pl.semaphore_wait(barrier, n - 1 + ns - 1)

    def hop1(peer, src):
        return pltpu.make_async_remote_copy(
            src_ref=send1.at[peer], dst_ref=recv1.at[src], send_sem=s1.at[peer], recv_sem=r1.at[src],
            device_id=(peer, st), device_id_type=MESH)

    def hop1_keys(peer, src):
        return pltpu.make_async_remote_copy(
            src_ref=keys_out.at[peer], dst_ref=keys_in.at[src], send_sem=k1.at[peer], recv_sem=q1.at[src],
            device_id=(peer, st), device_id_type=MESH)

    def build(c):
        slots = jnp.broadcast_to(slot_ref[...] - c * 128, (128, count))
        pick = (slots == iota((128, count), 0)).astype(BF16)
        y = mm_nt(pick, rows_ref[...])
        tail = y[:, 128:256]
        send1[c, 0:CLASS_CAP, :] = y[0:CLASS_CAP, 0:128].astype(BF16)
        low = iota((64, 128), 1) < 64
        send1[c, CLASS_CAP:BLOCK, :] = jnp.where(low, tail[0:64], pltpu.roll(tail[64:128], 64, 1)).astype(BF16)
        turned = jnp.transpose(tail)
        keys_out[c] = (turned[64:65] * 64.0 + turned[65:66] - 64.0).astype(I32)

    def start1(t, _):
        c = cfd_peer(t)
        build(c)
        hop1(c, me).start()
        hop1_keys(c, me).start()
        return 0

    lax.fori_loop(1, n, start1, 0)
    build(me)
    recv1[me] = send1[me]
    keys_in[me] = keys_out[me]

    acc[...] = jnp.zeros_like(acc)

    def combine(g, _):
        keys, parts = [], []
        for u in range(4):
            t = g * 4 + u
            src = lax.rem(me + n - t, n)

            @pl.when(t > 0)
            def _():
                hop1(src, src).wait_recv()
                hop1_keys(src, src).wait_recv()

            keys.append(keys_in[src])
            parts.append(unpack(recv1[src]))
        keys = jnp.concatenate(keys, axis=1)
        parts = jnp.concatenate(parts, axis=0)

        def block(b, _):
            at = pl.ds(pl.multiple_of(b * 256, 256), 256)
            hit = jnp.broadcast_to(keys - b * 256, (256, 512)) == iota((256, 512), 0)
            acc[at, :] += mm(hit.astype(BF16), parts)
            return 0

        lax.fori_loop(0, acc.shape[0] // 256, block, 0)
        return 0

    lax.fori_loop(0, n // 4, combine, 0)

    def hop2(peer, src):
        return pltpu.make_async_remote_copy(
            src_ref=send2.at[peer], dst_ref=recv2.at[src], send_sem=s2.at[peer], recv_sem=r2.at[src],
            device_id=(peer, st), device_id_type=MESH)

    def pack2(d):
        at = pl.ds(pl.multiple_of(d * 64, 64), 64)
        send2[d, 0:64, :] = acc[at, 0:128].astype(BF16)
        tail = acc[at, 128:256]
        tail = tail + pltpu.roll(tail, 64, 1)
        low = iota((32, 128), 1) < 64
        send2[d, 64:96, :] = jnp.where(low, tail[0:32], tail[32:64]).astype(BF16)

    def start2(t, _):
        d = cfd_peer(t)
        pack2(d)
        hop2(d, me).start()
        return 0

    lax.fori_loop(1, n, start2, 0)
    pack2(me)
    recv2[me] = send2[me]

    mode_copy.wait()
    force[...] = jnp.zeros_like(force)

    def project(g, _):
        parts = []
        for u in range(4):
            b = g * 4 + u
            blk = n - 1 - b
            src = lax.rem(me + blk, n)

            @pl.when(blk > 0)
            def _():
                hop2(src, src).wait_recv()

            tail = recv2[src, 64:96, :]
            low = iota((32, 128), 1) < 64
            zero = jnp.zeros_like(tail)
            tail = jnp.concatenate([jnp.where(low, tail, zero), jnp.where(low, zero, tail)], axis=0)
            parts.append(jnp.concatenate([recv2[src, 0:64, :], tail], axis=1))
        load = jnp.concatenate(parts[::-1], axis=0)
        load = jnp.transpose(load.astype(F32)).astype(BF16)
        at = pl.ds(pl.multiple_of((n // 4 - 1 - g) * 256, 256), 256)
        f0 = mm(load[0:64], mode_v[0, at, :])
        f1 = mm(load[64:128], mode_v[1, at, :])
        f2 = mm(load[128:256], mode_v[2, at, :])
        force[...] += f0 + f1 + f2[0:64] + f2[64:128]
        return 0

    lax.fori_loop(0, n // 4, project, 0)

    for p in range(ns):
        piece_out[p] = force[8 * p : 8 * p + 8, :] + poison_ref[0:8, 0:1]

    def hop_a(q, dev, src):
        return pltpu.make_async_remote_copy(
            src_ref=piece_out.at[q], dst_ref=piece_in.at[src], send_sem=sa.at[q], recv_sem=ra.at[src],
            device_id=dev, device_id_type=MESH)

    def hop_y(y, dev, src):
        return pltpu.make_async_remote_copy(
            src_ref=col_out, dst_ref=col_in.at[src], send_sem=sy.at[y], recv_sem=ry.at[src],
            device_id=dev, device_id_type=MESH)

    def hop_b(z, dev, src):
        return pltpu.make_async_remote_copy(
            src_ref=ring_out, dst_ref=ring_in.at[src], send_sem=sb.at[z], recv_sem=rb.at[src],
            device_id=dev, device_id_type=MESH)

    def hop_c(q, dev, piece):
        return pltpu.make_async_remote_copy(
            src_ref=total_in.at[piece], dst_ref=total_in.at[piece], send_sem=sc.at[q], recv_sem=rc.at[piece],
            device_id=dev, device_id_type=MESH)

    def phase(hop, peer_of, size, mine):
        for t in range(1, size):
            k, dev = peer_of(t)
            hop(k, dev, mine).start()

    def arrive(hop, peer_of, size):
        for t in range(1, size):
            k, dev = peer_of(size - t)
            hop(k, dev, k).wait_recv()

    phase(hop_a, struct_peer, ns, st)
    piece_in[st] = piece_out[st]
    arrive(hop_a, struct_peer, ns)
    col_out[...] = jnp.sum(piece_in[...], axis=0)
    phase(hop_y, y_peer, ny, my_y)
    col_in[my_y] = col_out[...]
    arrive(hop_y, y_peer, ny)
    ring_out[...] = jnp.sum(col_in[...], axis=0)
    phase(hop_b, z_peer, nz, my_z)
    ring_in[my_z] = ring_out[...]
    arrive(hop_b, z_peer, nz)
    total_in[st] = jnp.sum(ring_in[...], axis=0)
    phase(hop_c, struct_peer, ns, st)
    arrive(hop_c, struct_peer, ns)
    whole = jnp.concatenate([total_in[p] for p in range(ns)], axis=0)
    amp_t = whole / (stiff_ref[...] * nodes_scale)
    amp_ref[...] = amp_t
    amp = jnp.transpose(jnp.concatenate([amp_t, amp_t], axis=0))
    both = amp.astype(BF16)
    low = iota(amp.shape, 1) < 64
    left = jnp.where(low, amp, 0.0).astype(BF16)
    right = jnp.where(low, 0.0, amp).astype(BF16)

    def hop3(peer, src):
        return pltpu.make_async_remote_copy(
            src_ref=send3.at[peer], dst_ref=recv3.at[src], send_sem=s3.at[peer], recv_sem=r3.at[src],
            device_id=(peer, st), device_id_type=MESH)

    def expand(g, _):
        at = pl.ds(pl.multiple_of(g * 256, 256), 256)
        d01 = (mm(mode_v[0, at, :], left) + mm(mode_v[1, at, :], right)).astype(BF16)
        d2 = mm(mode_v[2, at, :], both)
        for u in range(4):
            b = g * 4 + u
            peer = cfd_peer(b)
            send3[peer, 0:64, :] = d01[64 * u : 64 * u + 64]
            keep = iota((32, 128), 1) < 64
            send3[peer, 64:96, :] = jnp.where(
                keep, d2[64 * u : 64 * u + 32], d2[64 * u + 32 : 64 * u + 64]).astype(BF16)

            @pl.when(b > 0)
            def _():
                hop3(peer, me).start()

        return 0

    lax.fori_loop(0, n // 4, expand, 0)
    recv3[me] = send3[me]

    def unpack3(t, _):
        src = lax.rem(me + n - t, n)

        @pl.when(t > 0)
        def _():
            hop3(src, src).wait_recv()

        at = pl.multiple_of(src * 64, 64)
        disp[pl.ds(at, 64), 0:128] = recv3[src, 0:64, :]
        tail = recv3[src, 64:96, :].astype(F32)
        other = pltpu.roll(tail, 64, 1)
        keep = iota((32, 128), 1) < 64
        disp[pl.ds(at, 32), 128:256] = jnp.where(keep, tail, other).astype(BF16)
        disp[pl.ds(at + 32, 32), 128:256] = jnp.where(keep, other, tail).astype(BF16)
        return 0

    lax.fori_loop(0, n, unpack3, 0)

    def hop4(peer, src):
        return pltpu.make_async_remote_copy(
            src_ref=send4.at[peer], dst_ref=recv4.at[src], send_sem=s4.at[peer], recv_sem=r4.at[src],
            device_id=(peer, st), device_id_type=MESH)

    def gather(src):
        keys = column(keys_in[src].astype(F32)).astype(I32)
        lane = iota((128, 128), 1)
        pick = jnp.concatenate(
            [(keys - 128 * q == lane).astype(BF16) for q in range(disp.shape[0] // 128)], axis=1)
        y = mm(pick, disp[...])
        keep = iota((64, 128), 1) < 64
        send4[src, 0:CLASS_CAP, :] = y[0:CLASS_CAP, 0:128].astype(BF16)
        send4[src, CLASS_CAP:BLOCK, :] = jnp.where(keep, y[0:64, 128:256], y[64:128, 128:256]).astype(BF16)

    def start4(t, _):
        src = cfd_peer(t)
        gather(src)
        hop4(src, me).start()
        return 0

    lax.fori_loop(1, n, start4, 0)
    gather(me)
    recv4[me] = send4[me]

    acc_t[...] = jnp.zeros_like(acc_t)

    def place(g, _):
        parts, firsts = [], []
        for u in range(4):
            t = g * 4 + u
            src = lax.rem(me + n - t, n)

            @pl.when(t > 0)
            def _():
                hop4(src, src).wait_recv()

            firsts.append(src * 128)
            parts.append(unpack(recv4[src]))
        parts = jnp.concatenate(parts, axis=0)
        parts = jnp.transpose(parts.astype(F32)).astype(BF16)
        for b in range(count // 512):
            at = slice(512 * b, 512 * b + 512)
            slots = slot_ref[:, at]
            sub = iota((128, 512), 0)
            pick = jnp.concatenate(
                [(jnp.broadcast_to(slots - first, (128, 512)) == sub).astype(BF16) for first in firsts], axis=0)
            acc_t[:, at] += mm(parts, pick)
        return 0

    lax.fori_loop(0, n // 4, place, 0)
    weight = weight_ref[...]
    out_ref[0:128, :] = (acc_t[0:128, :] * weight).astype(BF16)
    out_ref[128:192, :] = ((acc_t[128:192, :] + acc_t[192:256, :]) * weight).astype(BF16)

    def sent(t, _):
        peer = cfd_peer(t)
        hop1(peer, me).wait_send()
        hop1_keys(peer, me).wait_send()
        hop2(peer, me).wait_send()
        hop3(peer, me).wait_send()
        hop4(peer, me).wait_send()
        return 0

    lax.fori_loop(1, n, sent, 0)

    for t in range(1, ns):
        q, dev = struct_peer(t)
        hop_a(q, dev, st).wait_send()
        hop_c(q, dev, st).wait_send()
    for t in range(1, ny):
        y, dev = y_peer(t)
        hop_y(y, dev, my_y).wait_send()
    for t in range(1, nz):
        z, dev = z_peer(t)
        hop_b(z, dev, my_z).wait_send()


def fast(node_loads, dest_owner, dest_elem, node_weight, mode_shapes, stiffness):
    rows, width = node_loads.shape
    n, ns = lax.axis_size("cfd"), lax.axis_size("struct")
    ny = 4
    nz = n // ny
    comps, elems, modes = mode_shapes.shape
    scale = float(np.sqrt(np.float32(3.0 * rows * n * ns)))
    vmem = pl.BlockSpec(memory_space=pltpu.VMEM)
    dma = pltpu.SemaphoreType.DMA
    pair = (n, BLOCK, 128)
    dense = (n, 96, 128)
    piece = (64 // ns, modes)
    out_t, amp_t = pl.pallas_call(
        functools.partial(fused_kernel, n, ny, ns, scale),
        out_shape=(jax.ShapeDtypeStruct((width, rows), BF16), jax.ShapeDtypeStruct((64, modes), F32)),
        in_specs=[vmem] * 5 + [pl.BlockSpec(memory_space=pl.ANY)],
        out_specs=(vmem, vmem),
        scratch_shapes=[
            pltpu.VMEM((256, rows), BF16), pltpu.VMEM((1, rows), I32), pltpu.VMEM((8, 128), F32),
            pltpu.VMEM(pair, BF16), pltpu.VMEM((n, 1, 128), I32),
            pltpu.VMEM(pair, BF16), pltpu.VMEM((n, 1, 128), I32),
            pltpu.VMEM((elems, 256), F32), pltpu.VMEM(dense, BF16), pltpu.VMEM(dense, BF16),
            pltpu.VMEM(mode_shapes.shape, BF16), pltpu.VMEM((64, modes), F32),
            pltpu.VMEM((ns,) + piece, F32), pltpu.VMEM((ns,) + piece, F32),
            pltpu.VMEM(piece, F32), pltpu.VMEM((ny,) + piece, F32),
            pltpu.VMEM(piece, F32), pltpu.VMEM((nz,) + piece, F32), pltpu.VMEM((ns,) + piece, F32),
            pltpu.VMEM(dense, BF16), pltpu.VMEM(dense, BF16), pltpu.VMEM((elems, 256), BF16),
            pltpu.VMEM(pair, BF16), pltpu.VMEM(pair, BF16), pltpu.VMEM((256, rows), F32),
            dma((n,)), dma((n,)), dma((n,)), dma((n,)), dma((n,)), dma((n,)),
            dma((ns,)), dma((ns,)), dma((ny,)), dma((ny,)), dma((nz,)), dma((nz,)), dma((ns,)), dma((ns,)),
            dma((n,)), dma((n,)), dma((n,)), dma((n,)), dma(()),
        ],
        compiler_params=pltpu.CompilerParams(
            collective_id=0, has_side_effects=True, vmem_limit_bytes=56 * 1024 * 1024),
        cost_estimate=pl.CostEstimate(flops=30_000_000_000, bytes_accessed=10_000_000, transcendentals=0),
    )(
        dest_owner.reshape(1, rows), dest_elem.reshape(1, rows), node_weight.reshape(1, rows),
        node_loads.T, stiffness.reshape(1, modes), mode_shapes,
    )
    return out_t.T, amp_t.T


def per_device(*args):
    node_disp, modal_amp = fast(*args)
    crowded = jnp.isnan(modal_amp[0, 0])
    return lax.cond(crowded, lambda a, f: general(*a), lambda a, f: f, args, (node_disp, modal_amp))


def solution(mesh):
    placed = (
        P(("cfd", "struct"), None),
        P(("cfd", "struct"), None),
        P(("cfd", "struct")),
        P(("cfd", "struct")),
        P(None, ("cfd", "struct"), None),
        P(),
    )
    return jax.shard_map(
        per_device,
        mesh=mesh,
        in_specs=placed,
        out_specs=(P(("cfd", "struct"), None), P()),
        check_vma=False,
    )
```

```python
import functools
import math

import jax
import jax.numpy as jnp
import numpy as np
from jax import lax
from jax.experimental import pallas as pl
from jax.experimental.pallas import tpu as pltpu
from jax.sharding import PartitionSpec as P

MESH = pl.DeviceIdType.MESH
BF16, F32, I32 = jnp.bfloat16, jnp.float32, jnp.int32
CLASS_CAP = 112


def general(node_loads, dest_owner, dest_elem, node_weight, mode_shapes, stiffness):
    rows, width = node_loads.shape
    rhs_count = width // 3
    owners = lax.axis_size("cfd")
    devices = owners * lax.axis_size("struct")
    capacity = max(2, 4 * rows // owners)
    elems = mode_shapes.shape[1]
    owner = dest_owner[:, 0]
    owner_hits = (owner[:, None] == jnp.arange(owners, dtype=jnp.int32)[None, :]).astype(jnp.int32)
    earlier = jnp.cumsum(owner_hits, axis=0) - owner_hits
    rank = jnp.sum(earlier * owner_hits, axis=1)
    send_loads = jnp.zeros((owners, capacity, width), jnp.bfloat16).at[owner, rank].set(node_loads)
    send_elem = jnp.full((owners, capacity), elems, jnp.int32).at[owner, rank].set(dest_elem)
    got_loads, got_elem = (
        lax.all_to_all(send_loads, "cfd", split_axis=0, concat_axis=0, tiled=True),
        lax.all_to_all(send_elem, "cfd", split_axis=0, concat_axis=0, tiled=True),
    )
    slots = owners * capacity
    slot_loads = got_loads.reshape(slots, width)
    slot_elem = got_elem.reshape(slots)
    block = math.gcd(512, slots)
    columns = jnp.arange(elems, dtype=jnp.int32)

    def add_block(total, index):
        start = index * block
        loads = lax.dynamic_slice_in_dim(slot_loads, start, block, 0)
        target = lax.dynamic_slice_in_dim(slot_elem, start, block, 0)
        select = (columns[:, None] == target[None, :]).astype(jnp.bfloat16)
        return (total + jnp.dot(select, loads, preferred_element_type=jnp.float32), None)

    elem_sum, _ = lax.scan(
        add_block,
        jnp.zeros((elems, width), jnp.float32),
        jnp.arange(slots // block, dtype=jnp.int32),
    )
    elem_load = elem_sum.astype(jnp.bfloat16).reshape(elems, 3, rhs_count)
    partial_force = jnp.einsum(
        "kem,ekr->mr", mode_shapes, elem_load, preferred_element_type=jnp.float32
    )
    scale = jnp.sqrt(jnp.float32(3.0 * rows * devices))
    pieces = partial_force.reshape(devices, 1, -1)
    pieces = lax.all_to_all(pieces, ("cfd", "struct"), split_axis=0, concat_axis=0, tiled=True)
    piece = jnp.broadcast_to(jnp.sum(pieces, axis=0, keepdims=True), pieces.shape)
    pieces = lax.all_to_all(piece, ("cfd", "struct"), split_axis=0, concat_axis=0, tiled=True)
    modal_force = pieces.reshape(partial_force.shape)
    modal_amp = modal_force / (stiffness[:, None] * scale)
    amp_low = modal_amp.astype(jnp.bfloat16)
    elem_disp = jnp.einsum("kem,mr->ekr", mode_shapes, amp_low, preferred_element_type=jnp.float32)
    elem_disp = elem_disp.reshape(elems, width).astype(jnp.bfloat16)
    slot_disp = jnp.take(elem_disp, slot_elem, axis=0, mode="fill", fill_value=0).reshape(
        owners, capacity, width
    )
    returned = lax.all_to_all(slot_disp, "cfd", split_axis=0, concat_axis=0, tiled=True)
    node_value = returned[owner, rank]
    node_disp = (node_weight[:, None] * node_value.astype(jnp.float32)).astype(jnp.bfloat16)
    return (node_disp, modal_amp)


def mm(a, b):
    return jnp.dot(a, b, preferred_element_type=F32)


def mm_nt(a, b):
    return lax.dot_general(a, b, (((1,), (1,)), ((), ())), preferred_element_type=F32)


def iota(shape, dim):
    return lax.broadcasted_iota(I32, shape, dim)


def chosen(row, value, tall):
    few = (jnp.broadcast_to(row, (16, row.shape[1])) == value).astype(F32).astype(BF16)
    return jnp.concatenate([few] * (tall // 16), axis=0)


def one_hot(row, tall):
    return (jnp.broadcast_to(row, (tall, row.shape[1])) == iota((tall, row.shape[1]), 0)).astype(F32).astype(BF16)


def column(row):
    return jnp.transpose(jnp.broadcast_to(row, (128, 128)))


def split_halves(tail):
    low = iota(tail.shape, 1) < 64
    zero = jnp.zeros_like(tail)
    return jnp.concatenate([jnp.where(low, tail, zero), jnp.where(low, zero, tail)], axis=0)


def padded(head):
    return jnp.concatenate([head, jnp.zeros((128 - CLASS_CAP, 128), BF16)], axis=0)


def fused_kernel(
    n, ny, ns, nodes_scale,
    owner_ref, elem_ref, weight_ref, loads_ref, stiff_ref, mode_ref,
    out_ref, amp_ref,
    rows_ref, slot_ref, poison_ref, keys_out, keys_in, acc, acc_t,
    send1, recv1, send2, recv2, send3, recv3, send4, recv4,
    send1t, recv1t, send2t, recv2t, send3t, recv3t, send4t, recv4t,
    mode_v, force, piece_out, piece_in, col_out, col_in, ring_out, ring_in, total_in, disp, picks, base_ref,
    s1, r1, s2, r2, s3, r3, s4, r4, s1t, r1t, s2t, r2t, s3t, r3t, s4t, r4t,
    k1, q1, sa, ra, sy, ry, sb, rb, sc, rc, mode_sem,
):
    nz = n // ny
    me = lax.axis_index("cfd")
    st = lax.axis_index("struct")
    my_y, my_z = me // nz, lax.rem(me, nz)
    count = rows_ref.shape[1]

    def cfd_peer(t):
        return lax.rem(me + t, n)

    def struct_peer(t):
        q = lax.rem(st + t, ns)
        return q, (me, q)

    def y_peer(t):
        y = lax.rem(my_y + t, ny)
        return y, (y * nz + my_z, st)

    def hop_of(out, into, send, recv):
        def hop(peer, src):
            return pltpu.make_async_remote_copy(
                src_ref=out.at[peer], dst_ref=into.at[src], send_sem=send.at[peer], recv_sem=recv.at[src],
                device_id=(peer, st), device_id_type=MESH)

        return hop

    hop1, hop1t = hop_of(send1, recv1, s1, r1), hop_of(send1t, recv1t, s1t, r1t)
    hop2, hop2t = hop_of(send2, recv2, s2, r2), hop_of(send2t, recv2t, s2t, r2t)
    hop3, hop3t = hop_of(send3, recv3, s3, r3), hop_of(send3t, recv3t, s3t, r3t)
    hop4, hop4t = hop_of(send4, recv4, s4, r4), hop_of(send4t, recv4t, s4t, r4t)
    hop1_keys = hop_of(keys_out, keys_in, k1, q1)

    def z_peer(t):
        z = lax.rem(my_z + t, nz)
        return z, (my_y * nz + z, st)

    barrier = pltpu.get_barrier_semaphore()

    def greet_cfd(t, _):
        pl.semaphore_signal(barrier, inc=1, device_id=(cfd_peer(t), st), device_id_type=MESH)
        return 0

    def greet_struct(t, _):
        _, dev = struct_peer(t)
        pl.semaphore_signal(barrier, inc=1, device_id=dev, device_id_type=MESH)
        return 0

    lax.fori_loop(1, n, greet_cfd, 0)
    lax.fori_loop(1, ns, greet_struct, 0)
    mode_copy = pltpu.make_async_copy(mode_ref, mode_v, mode_sem)
    mode_copy.start()

    owner = owner_ref[...]
    elem = elem_ref[...]
    cls = ((elem >> 6) + owner) & (n - 1)
    upper = (iota((256, 256), 0) < iota((256, 256), 1)).astype(BF16)
    base = jnp.zeros((n, 1), F32)
    for q in range(count // 256):
        part = cls[:, 256 * q : 256 * q + 256]
        hit = iota((n, 256), 0) == jnp.broadcast_to(part, (n, 256))
        hit_f = hit.astype(F32)
        before = mm(hit_f.astype(BF16), upper) + base
        rank = jnp.sum(jnp.where(hit, before, 0.0), axis=0, keepdims=True).astype(I32)
        slot_ref[:, 256 * q : 256 * q + 256] = jnp.where(rank < CLASS_CAP, part * 128 + rank, -1)
        base = base + jnp.sum(hit_f, axis=1, keepdims=True)
    most = jnp.max(base, axis=0, keepdims=True)
    poison_ref[...] = jnp.broadcast_to(jnp.where(most > CLASS_CAP, jnp.nan, 0.0), (8, 128))

    sub = iota((64, count), 0)
    own = jnp.broadcast_to(owner + 1, (64, count))
    low_elem = jnp.broadcast_to(elem & 63, (64, count))
    rows_ref[0:192, :] = loads_ref[...]
    rows_ref[192:256, :] = jnp.where(sub == 0, own, jnp.where(sub == 1, low_elem, 0)).astype(F32).astype(BF16)

    base_ref[...] = one_hot(slot_ref[...] & 127, 128)
    pl.semaphore_wait(barrier, n - 1 + ns - 1)

    def build(g, _):
        classes = [cfd_peer(g * 4 + u) for u in range(4)]
        wanted = slot_ref[...] >> 7
        pick = jnp.concatenate([base_ref[...] * chosen(wanted, c, 128) for c in classes], axis=0)
        y4 = mm_nt(pick, rows_ref[...])
        low = iota((64, 128), 1) < 64
        for u, c in enumerate(classes):
            y = y4[128 * u : 128 * u + 128]
            tail = y[:, 128:256]
            send1[c] = y[0:CLASS_CAP, 0:128].astype(BF16)
            send1t[c] = jnp.where(low, tail[0:64], pltpu.roll(tail[64:128], 64, 1)).astype(BF16)
            turned = jnp.transpose(tail)
            keys_out[c] = (turned[64:65] * 64.0 + turned[65:66] - 64.0).astype(I32)

            @pl.when(g * 4 + u > 0)
            def _():
                hop1(c, me).start()
                hop1_keys(c, me).start()

        return 0

    def start1_tail(t, _):
        hop1t(cfd_peer(t), me).start()
        return 0

    lax.fori_loop(0, n // 4, build, 0)
    lax.fori_loop(1, n, start1_tail, 0)
    recv1[me] = send1[me]
    recv1t[me] = send1t[me]
    keys_in[me] = keys_out[me]

    acc[...] = jnp.zeros_like(acc)

    def combine(g, hops, part, first):
        keys, parts = [], []
        for u in range(4):
            t = g * 4 + u
            src = lax.rem(me + n - t, n)

            @pl.when(t > 0)
            def _():
                for hop in hops:
                    hop(src, src).wait_recv()

            keys.append(keys_in[src])
            parts.append(part(src))
        keys = jnp.concatenate(keys, axis=1)
        parts = jnp.concatenate(parts, axis=0)
        low_hit = one_hot(keys & 255, 256)

        hit = jnp.concatenate([low_hit * chosen(keys >> 8, b, 256) for b in range(acc.shape[0] // 256)], axis=0)
        acc[:, first : first + 128] += mm(hit, parts)
        return 0

    def pack2(d):
        at = pl.ds(pl.multiple_of(d * 64, 64), 64)
        send2[d] = acc[at, 0:128].astype(BF16)

    def pack2_tail(d):
        at = pl.ds(pl.multiple_of(d * 64, 64), 64)
        tail = acc[at, 128:256]
        tail = tail + pltpu.roll(tail, 64, 1)
        low = iota((32, 128), 1) < 64
        send2t[d] = jnp.where(low, tail[0:32], tail[32:64]).astype(BF16)

    def start2(t, _):
        d = cfd_peer(t)
        pack2(d)
        hop2(d, me).start()
        return 0

    def start2_tail(t, _):
        d = cfd_peer(t)
        pack2_tail(d)
        hop2t(d, me).start()
        return 0

    lax.fori_loop(0, n // 4, lambda g, _: combine(g, (hop1, hop1_keys), lambda src: padded(recv1[src]), 0), 0)
    lax.fori_loop(1, n, start2, 0)
    pack2(me)
    recv2[me] = send2[me]
    lax.fori_loop(0, n // 4, lambda g, _: combine(g, (hop1t,), lambda src: split_halves(recv1t[src]), 128), 0)
    lax.fori_loop(1, n, start2_tail, 0)
    pack2_tail(me)
    recv2t[me] = send2t[me]

    mode_copy.wait()
    force[...] = jnp.zeros_like(force)

    def project(g, hop, part):
        parts = []
        for u in range(4):
            blk = n - 1 - (g * 4 + u)
            src = lax.rem(me + blk, n)

            @pl.when(blk > 0)
            def _():
                hop(src, src).wait_recv()

            parts.append(part(src))
        load = jnp.concatenate(parts[::-1], axis=0)
        return jnp.transpose(load.astype(F32)).astype(BF16), pl.ds(pl.multiple_of((n // 4 - 1 - g) * 256, 256), 256)

    def project_head(g, _):
        load, at = project(g, hop2, lambda src: recv2[src])
        force[...] += mm(load[0:64], mode_v[0, at, :]) + mm(load[64:128], mode_v[1, at, :])
        return 0

    def tail_of(src):
        tail = recv2t[src]
        low = iota((32, 128), 1) < 64
        zero = jnp.zeros_like(tail)
        return jnp.concatenate([jnp.where(low, tail, zero), jnp.where(low, zero, tail)], axis=0)

    def project_tail(g, _):
        load, at = project(g, hop2t, tail_of)
        f2 = mm(load, mode_v[2, at, :])
        force[...] += f2[0:64] + f2[64:128]
        return 0

    lax.fori_loop(0, n // 4, project_head, 0)
    lax.fori_loop(0, n // 4, project_tail, 0)

    for p in range(ns):
        piece_out[p] = force[8 * p : 8 * p + 8, :] + poison_ref[0:8, 0:1]

    def hop_a(q, dev, src):
        return pltpu.make_async_remote_copy(
            src_ref=piece_out.at[q], dst_ref=piece_in.at[src], send_sem=sa.at[q], recv_sem=ra.at[src],
            device_id=dev, device_id_type=MESH)

    def hop_y(y, dev, src):
        return pltpu.make_async_remote_copy(
            src_ref=col_out, dst_ref=col_in.at[src], send_sem=sy.at[y], recv_sem=ry.at[src],
            device_id=dev, device_id_type=MESH)

    def hop_b(z, dev, src):
        return pltpu.make_async_remote_copy(
            src_ref=ring_out, dst_ref=ring_in.at[src], send_sem=sb.at[z], recv_sem=rb.at[src],
            device_id=dev, device_id_type=MESH)

    def hop_c(q, dev, piece):
        return pltpu.make_async_remote_copy(
            src_ref=total_in.at[piece], dst_ref=total_in.at[piece], send_sem=sc.at[q], recv_sem=rc.at[piece],
            device_id=dev, device_id_type=MESH)

    def phase(hop, peer_of, size, mine):
        for t in range(1, size):
            k, dev = peer_of(t)
            hop(k, dev, mine).start()

    def arrive(hop, peer_of, size):
        for t in range(1, size):
            k, dev = peer_of(size - t)
            hop(k, dev, k).wait_recv()

    phase(hop_a, struct_peer, ns, st)
    piece_in[st] = piece_out[st]
    arrive(hop_a, struct_peer, ns)
    col_out[...] = jnp.sum(piece_in[...], axis=0)
    phase(hop_y, y_peer, ny, my_y)
    col_in[my_y] = col_out[...]
    arrive(hop_y, y_peer, ny)
    ring_out[...] = jnp.sum(col_in[...], axis=0)
    phase(hop_b, z_peer, nz, my_z)
    ring_in[my_z] = ring_out[...]
    arrive(hop_b, z_peer, nz)
    total_in[st] = jnp.sum(ring_in[...], axis=0)
    phase(hop_c, struct_peer, ns, st)
    arrive(hop_c, struct_peer, ns)
    whole = jnp.concatenate([total_in[p] for p in range(ns)], axis=0)
    amp_t = whole / (stiff_ref[...] * nodes_scale)
    amp_ref[...] = amp_t
    amp = jnp.transpose(jnp.concatenate([amp_t, amp_t], axis=0))
    both = amp.astype(BF16)
    low = iota(amp.shape, 1) < 64
    left = jnp.where(low, amp, 0.0).astype(BF16)
    right = jnp.where(low, 0.0, amp).astype(BF16)

    def expand(g, _):
        at = pl.ds(pl.multiple_of(g * 256, 256), 256)
        d01 = (mm(mode_v[0, at, :], left) + mm(mode_v[1, at, :], right)).astype(BF16)
        for u in range(4):
            b = g * 4 + u
            peer = cfd_peer(b)
            send3[peer] = d01[64 * u : 64 * u + 64]

            @pl.when(b > 0)
            def _():
                hop3(peer, me).start()

        return 0

    def expand_tail(g, _):
        at = pl.ds(pl.multiple_of(g * 256, 256), 256)
        d2 = mm(mode_v[2, at, :], both)
        keep = iota((32, 128), 1) < 64
        for u in range(4):
            b = g * 4 + u
            peer = cfd_peer(b)
            send3t[peer] = jnp.where(keep, d2[64 * u : 64 * u + 32], d2[64 * u + 32 : 64 * u + 64]).astype(BF16)

            @pl.when(b > 0)
            def _():
                hop3t(peer, me).start()

        return 0

    lax.fori_loop(0, n // 4, expand, 0)
    lax.fori_loop(0, n // 4, expand_tail, 0)
    recv3[me] = send3[me]
    recv3t[me] = send3t[me]

    def choose(src, _):
        keys = column(keys_in[src].astype(F32)).astype(I32)
        low_hit = (keys & 127 == iota((128, 128), 1)).astype(F32).astype(BF16)
        high = (keys >> 7).astype(F32).astype(BF16)
        for q in range(disp.shape[0] // 128):
            picks[src, :, 128 * q : 128 * q + 128] = jnp.where(high == q, low_hit, jnp.zeros_like(low_hit))
        return 0

    lax.fori_loop(0, n, choose, 0)

    def unpack3(t, _):
        src = lax.rem(me + n - t, n)

        @pl.when(t > 0)
        def _():
            hop3(src, src).wait_recv()

        disp[pl.ds(pl.multiple_of(src * 64, 64), 64), 0:128] = recv3[src]
        return 0

    def unpack3_tail(t, _):
        src = lax.rem(me + n - t, n)

        @pl.when(t > 0)
        def _():
            hop3t(src, src).wait_recv()

        at = pl.multiple_of(src * 64, 64)
        tail = recv3t[src].astype(F32)
        other = pltpu.roll(tail, 64, 1)
        keep = iota((32, 128), 1) < 64
        disp[pl.ds(at, 32), 128:256] = jnp.where(keep, tail, other).astype(BF16)
        disp[pl.ds(at + 32, 32), 128:256] = jnp.where(keep, other, tail).astype(BF16)
        return 0

    def gather(g, _):
        sources = [cfd_peer(g * 4 + u) for u in range(4)]
        y4 = mm(jnp.concatenate([picks[src] for src in sources], axis=0), disp[:, 0:128])
        for u, src in enumerate(sources):
            send4[src] = y4[128 * u : 128 * u + CLASS_CAP].astype(BF16)

            @pl.when(g * 4 + u > 0)
            def _():
                hop4(src, me).start()

        return 0

    def gather_tail(g, _):
        sources = [cfd_peer(g * 4 + u) for u in range(4)]
        y4 = mm(jnp.concatenate([picks[src] for src in sources], axis=0), disp[:, 128:256])
        keep = iota((64, 128), 1) < 64
        for u, src in enumerate(sources):
            y = y4[128 * u : 128 * u + 128]
            send4t[src] = jnp.where(keep, y[0:64], y[64:128]).astype(BF16)

            @pl.when(g * 4 + u > 0)
            def _():
                hop4t(src, me).start()

        return 0

    lax.fori_loop(0, n, unpack3, 0)
    lax.fori_loop(0, n // 4, gather, 0)
    recv4[me] = send4[me]
    lax.fori_loop(0, n, unpack3_tail, 0)
    lax.fori_loop(0, n // 4, gather_tail, 0)
    recv4t[me] = send4t[me]

    acc_t[...] = jnp.zeros_like(acc_t)

    def place(g, hop, part, first_row):
        parts, firsts = [], []
        for u in range(4):
            t = g * 4 + u
            src = lax.rem(me + n - t, n)

            @pl.when(t > 0)
            def _():
                hop(src, src).wait_recv()

            firsts.append(src)
            parts.append(part(src))
        parts = jnp.concatenate(parts, axis=0)
        parts = jnp.transpose(parts.astype(F32)).astype(BF16)
        for b in range(count // 512):
            at = slice(512 * b, 512 * b + 512)
            classes = slot_ref[:, at] >> 7
            base = base_ref[:, at]
            pick = jnp.concatenate([base * chosen(classes, first, 128) for first in firsts], axis=0)
            acc_t[first_row : first_row + 128, at] += mm(parts, pick)
        return 0

    lax.fori_loop(0, n // 4, lambda g, _: place(g, hop4, lambda src: padded(recv4[src]), 0), 0)
    lax.fori_loop(0, n // 4, lambda g, _: place(g, hop4t, lambda src: split_halves(recv4t[src]), 128), 0)
    weight = weight_ref[...]
    out_ref[0:128, :] = (acc_t[0:128, :] * weight).astype(BF16)
    out_ref[128:192, :] = ((acc_t[128:192, :] + acc_t[192:256, :]) * weight).astype(BF16)

    def sent(t, _):
        peer = cfd_peer(t)
        for hop in (hop1, hop1t, hop1_keys, hop2, hop2t, hop3, hop3t, hop4, hop4t):
            hop(peer, me).wait_send()
        return 0

    lax.fori_loop(1, n, sent, 0)

    for t in range(1, ns):
        q, dev = struct_peer(t)
        hop_a(q, dev, st).wait_send()
        hop_c(q, dev, st).wait_send()
    for t in range(1, ny):
        y, dev = y_peer(t)
        hop_y(y, dev, my_y).wait_send()
    for t in range(1, nz):
        z, dev = z_peer(t)
        hop_b(z, dev, my_z).wait_send()


def fast(node_loads, dest_owner, dest_elem, node_weight, mode_shapes, stiffness):
    rows, width = node_loads.shape
    n, ns = lax.axis_size("cfd"), lax.axis_size("struct")
    ny = 4
    nz = n // ny
    comps, elems, modes = mode_shapes.shape
    scale = float(np.sqrt(np.float32(3.0 * rows * n * ns)))
    vmem = pl.BlockSpec(memory_space=pltpu.VMEM)
    dma = pltpu.SemaphoreType.DMA
    head, tail = (n, CLASS_CAP, 128), (n, 64, 128)
    dense, dense_tail = (n, 64, 128), (n, 32, 128)
    piece = (64 // ns, modes)
    out_t, amp_t = pl.pallas_call(
        functools.partial(fused_kernel, n, ny, ns, scale),
        out_shape=(jax.ShapeDtypeStruct((width, rows), BF16), jax.ShapeDtypeStruct((64, modes), F32)),
        in_specs=[vmem] * 5 + [pl.BlockSpec(memory_space=pl.ANY)],
        out_specs=(vmem, vmem),
        scratch_shapes=[
            pltpu.VMEM((256, rows), BF16), pltpu.VMEM((1, rows), I32), pltpu.VMEM((8, 128), F32),
            pltpu.VMEM((n, 1, 128), I32), pltpu.VMEM((n, 1, 128), I32),
            pltpu.VMEM((elems, 256), F32), pltpu.VMEM((256, rows), F32),
            *(pltpu.VMEM(v, BF16) for v in (head, head, dense, dense, dense, dense, head, head)),
            *(pltpu.VMEM(v, BF16) for v in (tail, tail, dense_tail, dense_tail, dense_tail, dense_tail, tail, tail)),
            pltpu.VMEM(mode_shapes.shape, BF16), pltpu.VMEM((64, modes), F32),
            pltpu.VMEM((ns,) + piece, F32), pltpu.VMEM((ns,) + piece, F32),
            pltpu.VMEM(piece, F32), pltpu.VMEM((ny,) + piece, F32),
            pltpu.VMEM(piece, F32), pltpu.VMEM((nz,) + piece, F32), pltpu.VMEM((ns,) + piece, F32),
            pltpu.VMEM((elems, 256), BF16), pltpu.VMEM((n, 128, elems), BF16), pltpu.VMEM((128, rows), BF16),
            *(dma((n,)) for _ in range(18)),
            dma((ns,)), dma((ns,)), dma((ny,)), dma((ny,)), dma((nz,)), dma((nz,)), dma((ns,)), dma((ns,)),
            dma(()),
        ],
        compiler_params=pltpu.CompilerParams(
            collective_id=0, has_side_effects=True, vmem_limit_bytes=56 * 1024 * 1024),
        cost_estimate=pl.CostEstimate(flops=30_000_000_000, bytes_accessed=10_000_000, transcendentals=0),
    )(
        dest_owner.reshape(1, rows), dest_elem.reshape(1, rows), node_weight.reshape(1, rows),
        node_loads.T, stiffness.reshape(1, modes), mode_shapes,
    )
    return out_t.T, amp_t.T


def per_device(*args):
    node_disp, modal_amp = fast(*args)
    crowded = jnp.isnan(modal_amp[0, 0])
    return lax.cond(crowded, lambda a, f: general(*a), lambda a, f: f, args, (node_disp, modal_amp))


def solution(mesh):
    placed = (
        P(("cfd", "struct"), None),
        P(("cfd", "struct"), None),
        P(("cfd", "struct")),
        P(("cfd", "struct")),
        P(None, ("cfd", "struct"), None),
        P(),
    )
    return jax.shard_map(
        per_device,
        mesh=mesh,
        in_specs=placed,
        out_specs=(P(("cfd", "struct"), None), P()),
        check_vma=False,
    )
```

```python
import functools
import math

import jax
import jax.numpy as jnp
import numpy as np
from jax import lax
from jax.experimental import pallas as pl
from jax.experimental.pallas import tpu as pltpu
from jax.sharding import PartitionSpec as P

MESH = pl.DeviceIdType.MESH
BF16, F32, I32 = jnp.bfloat16, jnp.float32, jnp.int32
CLASS_CAP = 112


def general(node_loads, dest_owner, dest_elem, node_weight, mode_shapes, stiffness):
    rows, width = node_loads.shape
    rhs_count = width // 3
    owners = lax.axis_size("cfd")
    devices = owners * lax.axis_size("struct")
    capacity = max(2, 4 * rows // owners)
    elems = mode_shapes.shape[1]
    owner = dest_owner[:, 0]
    owner_hits = (owner[:, None] == jnp.arange(owners, dtype=jnp.int32)[None, :]).astype(jnp.int32)
    earlier = jnp.cumsum(owner_hits, axis=0) - owner_hits
    rank = jnp.sum(earlier * owner_hits, axis=1)
    send_loads = jnp.zeros((owners, capacity, width), jnp.bfloat16).at[owner, rank].set(node_loads)
    send_elem = jnp.full((owners, capacity), elems, jnp.int32).at[owner, rank].set(dest_elem)
    got_loads, got_elem = (
        lax.all_to_all(send_loads, "cfd", split_axis=0, concat_axis=0, tiled=True),
        lax.all_to_all(send_elem, "cfd", split_axis=0, concat_axis=0, tiled=True),
    )
    slots = owners * capacity
    slot_loads = got_loads.reshape(slots, width)
    slot_elem = got_elem.reshape(slots)
    block = math.gcd(512, slots)
    columns = jnp.arange(elems, dtype=jnp.int32)

    def add_block(total, index):
        start = index * block
        loads = lax.dynamic_slice_in_dim(slot_loads, start, block, 0)
        target = lax.dynamic_slice_in_dim(slot_elem, start, block, 0)
        select = (columns[:, None] == target[None, :]).astype(jnp.bfloat16)
        return (total + jnp.dot(select, loads, preferred_element_type=jnp.float32), None)

    elem_sum, _ = lax.scan(
        add_block,
        jnp.zeros((elems, width), jnp.float32),
        jnp.arange(slots // block, dtype=jnp.int32),
    )
    elem_load = elem_sum.astype(jnp.bfloat16).reshape(elems, 3, rhs_count)
    partial_force = jnp.einsum(
        "kem,ekr->mr", mode_shapes, elem_load, preferred_element_type=jnp.float32
    )
    scale = jnp.sqrt(jnp.float32(3.0 * rows * devices))
    pieces = partial_force.reshape(devices, 1, -1)
    pieces = lax.all_to_all(pieces, ("cfd", "struct"), split_axis=0, concat_axis=0, tiled=True)
    piece = jnp.broadcast_to(jnp.sum(pieces, axis=0, keepdims=True), pieces.shape)
    pieces = lax.all_to_all(piece, ("cfd", "struct"), split_axis=0, concat_axis=0, tiled=True)
    modal_force = pieces.reshape(partial_force.shape)
    modal_amp = modal_force / (stiffness[:, None] * scale)
    amp_low = modal_amp.astype(jnp.bfloat16)
    elem_disp = jnp.einsum("kem,mr->ekr", mode_shapes, amp_low, preferred_element_type=jnp.float32)
    elem_disp = elem_disp.reshape(elems, width).astype(jnp.bfloat16)
    slot_disp = jnp.take(elem_disp, slot_elem, axis=0, mode="fill", fill_value=0).reshape(
        owners, capacity, width
    )
    returned = lax.all_to_all(slot_disp, "cfd", split_axis=0, concat_axis=0, tiled=True)
    node_value = returned[owner, rank]
    node_disp = (node_weight[:, None] * node_value.astype(jnp.float32)).astype(jnp.bfloat16)
    return (node_disp, modal_amp)


def mm(a, b):
    return jnp.dot(a, b, preferred_element_type=F32)


def mm_nt(a, b):
    return lax.dot_general(a, b, (((1,), (1,)), ((), ())), preferred_element_type=F32)


def iota(shape, dim):
    return lax.broadcasted_iota(I32, shape, dim)


def chosen(row, value, tall):
    few = (jnp.broadcast_to(row, (16, row.shape[1])) == value).astype(F32).astype(BF16)
    return jnp.concatenate([few] * (tall // 16), axis=0)


def one_hot(row, tall):
    return (jnp.broadcast_to(row, (tall, row.shape[1])) == iota((tall, row.shape[1]), 0)).astype(F32).astype(BF16)


def column(row):
    return jnp.transpose(jnp.broadcast_to(row, (128, 128)))


def split_halves(tail):
    low = iota(tail.shape, 1) < 64
    zero = jnp.zeros_like(tail)
    return jnp.concatenate([jnp.where(low, tail, zero), jnp.where(low, zero, tail)], axis=0)


def padded(head):
    return jnp.concatenate([head, jnp.zeros((128 - CLASS_CAP, 128), BF16)], axis=0)


def fused_kernel(
    n, ny, ns, nodes_scale,
    owner_ref, elem_ref, weight_ref, loads_ref, stiff_ref, mode_ref,
    out_ref, amp_ref,
    rows_ref, slot_ref, poison_ref, keys_out, keys_in, acc, acc_t,
    send1, recv1, send2, recv2, send3, recv3, send4, recv4,
    send1t, recv1t, send2t, recv2t, send3t, recv3t, send4t, recv4t,
    mode_v, force, piece_out, piece_in, col_out, col_in, ring_out, ring_in, total_in, disp, picks, base_ref,
    s1, r1, s2, r2, s3, r3, s4, r4, s1t, r1t, s2t, r2t, s3t, r3t, s4t, r4t,
    k1, q1, sa, ra, sy, ry, sb, rb, sc, rc, mode_sem,
):
    nz = n // ny
    me = lax.axis_index("cfd")
    st = lax.axis_index("struct")
    my_y, my_z = me // nz, lax.rem(me, nz)
    count = rows_ref.shape[1]

    def cfd_peer(t):
        return lax.rem(me + t, n)

    def struct_peer(t):
        q = lax.rem(st + t, ns)
        return q, (me, q)

    def y_peer(t):
        y = lax.rem(my_y + t, ny)
        return y, (y * nz + my_z, st)

    def hop_of(out, into, send, recv):
        def hop(peer, src):
            return pltpu.make_async_remote_copy(
                src_ref=out.at[peer], dst_ref=into.at[src], send_sem=send.at[peer], recv_sem=recv.at[src],
                device_id=(peer, st), device_id_type=MESH)

        return hop

    hop1, hop1t = hop_of(send1, recv1, s1, r1), hop_of(send1t, recv1t, s1t, r1t)
    hop2, hop2t = hop_of(send2, recv2, s2, r2), hop_of(send2t, recv2t, s2t, r2t)
    hop3, hop3t = hop_of(send3, recv3, s3, r3), hop_of(send3t, recv3t, s3t, r3t)
    hop4, hop4t = hop_of(send4, recv4, s4, r4), hop_of(send4t, recv4t, s4t, r4t)
    hop1_keys = hop_of(keys_out, keys_in, k1, q1)

    def z_peer(t):
        z = lax.rem(my_z + t, nz)
        return z, (my_y * nz + z, st)

    barrier = pltpu.get_barrier_semaphore()

    def greet_cfd(t, _):
        pl.semaphore_signal(barrier, inc=1, device_id=(cfd_peer(t), st), device_id_type=MESH)
        return 0

    def greet_struct(t, _):
        _, dev = struct_peer(t)
        pl.semaphore_signal(barrier, inc=1, device_id=dev, device_id_type=MESH)
        return 0

    lax.fori_loop(1, n, greet_cfd, 0)
    lax.fori_loop(1, ns, greet_struct, 0)
    mode_copy = pltpu.make_async_copy(mode_ref, mode_v, mode_sem)
    mode_copy.start()

    owner = owner_ref[...]
    elem = elem_ref[...]
    cls = ((elem >> 6) + owner) & (n - 1)
    upper = (iota((256, 256), 0) < iota((256, 256), 1)).astype(BF16)
    parts = [slice(256 * q, 256 * q + 256) for q in range(count // 256)]
    hits = [one_hot(cls[:, part], n) for part in parts]
    hits = jnp.concatenate(hits, axis=0)
    before = mm(hits, upper)
    hits = hits.astype(F32)
    sums = jnp.sum(hits, axis=1, keepdims=True)
    base = jnp.zeros((n, 1), F32)
    for q, part in enumerate(parts):
        own = slice(n * q, n * q + n)
        rank = jnp.sum(hits[own] * (before[own] + base), axis=0, keepdims=True).astype(I32)
        slot_ref[:, part] = jnp.where(rank < CLASS_CAP, cls[:, part] * 128 + rank, -1)
        base = base + sums[own]
    most = jnp.max(base, axis=0, keepdims=True)
    poison_ref[...] = jnp.broadcast_to(jnp.where(most > CLASS_CAP, jnp.nan, 0.0), (8, 128))

    sub = iota((64, count), 0)
    own = jnp.broadcast_to(owner + 1, (64, count))
    low_elem = jnp.broadcast_to(elem & 63, (64, count))
    rows_ref[0:192, :] = loads_ref[...]
    rows_ref[192:256, :] = jnp.where(sub == 0, own, jnp.where(sub == 1, low_elem, 0)).astype(F32).astype(BF16)

    base_ref[...] = one_hot(slot_ref[...] & 127, 128)
    pl.semaphore_wait(barrier, n - 1 + ns - 1)

    def build(g, _):
        classes = [cfd_peer(g * 4 + u) for u in range(4)]
        wanted = slot_ref[...] >> 7
        pick = jnp.concatenate([base_ref[...] * chosen(wanted, c, 128) for c in classes], axis=0)
        y4 = mm_nt(pick, rows_ref[...])
        low = iota((64, 128), 1) < 64
        for u, c in enumerate(classes):
            y = y4[128 * u : 128 * u + 128]
            tail = y[:, 128:256]
            send1[c] = y[0:CLASS_CAP, 0:128].astype(BF16)
            send1t[c] = jnp.where(low, tail[0:64], pltpu.roll(tail[64:128], 64, 1)).astype(BF16)
            turned = jnp.transpose(tail)
            keys_out[c] = (turned[64:65] * 64.0 + turned[65:66] - 64.0).astype(I32)

            @pl.when(g * 4 + u > 0)
            def _():
                hop1(c, me).start()
                hop1_keys(c, me).start()

        return 0

    def start1_tail(t, _):
        hop1t(cfd_peer(t), me).start()
        return 0

    lax.fori_loop(0, n // 4, build, 0)
    lax.fori_loop(1, n, start1_tail, 0)
    recv1[me] = send1[me]
    recv1t[me] = send1t[me]
    keys_in[me] = keys_out[me]

    acc[...] = jnp.zeros_like(acc)

    def combine(g, hops, part, first):
        keys, parts = [], []
        for u in range(4):
            t = g * 4 + u
            src = lax.rem(me + n - t, n)

            @pl.when(t > 0)
            def _():
                for hop in hops:
                    hop(src, src).wait_recv()

            keys.append(keys_in[src])
            parts.append(part(src))
        keys = jnp.concatenate(keys, axis=1)
        parts = jnp.concatenate(parts, axis=0)
        low_hit = one_hot(keys & 255, 256)

        hit = jnp.concatenate([low_hit * chosen(keys >> 8, b, 256) for b in range(acc.shape[0] // 256)], axis=0)
        acc[:, first : first + 128] += mm(hit, parts)
        return 0

    def pack2(d):
        at = pl.ds(pl.multiple_of(d * 64, 64), 64)
        send2[d] = acc[at, 0:128].astype(BF16)

    def pack2_tail(d):
        at = pl.ds(pl.multiple_of(d * 64, 64), 64)
        tail = acc[at, 128:256]
        tail = tail + pltpu.roll(tail, 64, 1)
        low = iota((32, 128), 1) < 64
        send2t[d] = jnp.where(low, tail[0:32], tail[32:64]).astype(BF16)

    def start2(t, _):
        d = cfd_peer(t)
        pack2(d)
        hop2(d, me).start()
        return 0

    def start2_tail(t, _):
        d = cfd_peer(t)
        pack2_tail(d)
        hop2t(d, me).start()
        return 0

    lax.fori_loop(0, n // 4, lambda g, _: combine(g, (hop1, hop1_keys), lambda src: padded(recv1[src]), 0), 0)
    lax.fori_loop(1, n, start2, 0)
    pack2(me)
    recv2[me] = send2[me]
    lax.fori_loop(0, n // 4, lambda g, _: combine(g, (hop1t,), lambda src: split_halves(recv1t[src]), 128), 0)
    lax.fori_loop(1, n, start2_tail, 0)
    pack2_tail(me)
    recv2t[me] = send2t[me]

    mode_copy.wait()
    force[...] = jnp.zeros_like(force)

    def project(g, hop, part):
        parts = []
        for u in range(4):
            blk = n - 1 - (g * 4 + u)
            src = lax.rem(me + blk, n)

            @pl.when(blk > 0)
            def _():
                hop(src, src).wait_recv()

            parts.append(part(src))
        load = jnp.concatenate(parts[::-1], axis=0)
        return jnp.transpose(load.astype(F32)).astype(BF16), pl.ds(pl.multiple_of((n // 4 - 1 - g) * 256, 256), 256)

    def project_head(g, _):
        load, at = project(g, hop2, lambda src: recv2[src])
        force[...] += mm(load[0:64], mode_v[0, at, :]) + mm(load[64:128], mode_v[1, at, :])
        return 0

    def tail_of(src):
        tail = recv2t[src]
        low = iota((32, 128), 1) < 64
        zero = jnp.zeros_like(tail)
        return jnp.concatenate([jnp.where(low, tail, zero), jnp.where(low, zero, tail)], axis=0)

    def project_tail(g, _):
        load, at = project(g, hop2t, tail_of)
        f2 = mm(load, mode_v[2, at, :])
        force[...] += f2[0:64] + f2[64:128]
        return 0

    lax.fori_loop(0, n // 4, project_head, 0)
    lax.fori_loop(0, n // 4, project_tail, 0)

    for p in range(ns):
        piece_out[p] = force[8 * p : 8 * p + 8, :] + poison_ref[0:8, 0:1]

    def hop_a(q, dev, src):
        return pltpu.make_async_remote_copy(
            src_ref=piece_out.at[q], dst_ref=piece_in.at[src], send_sem=sa.at[q], recv_sem=ra.at[src],
            device_id=dev, device_id_type=MESH)

    def hop_y(y, dev, src):
        return pltpu.make_async_remote_copy(
            src_ref=col_out, dst_ref=col_in.at[src], send_sem=sy.at[y], recv_sem=ry.at[src],
            device_id=dev, device_id_type=MESH)

    def hop_b(z, dev, src):
        return pltpu.make_async_remote_copy(
            src_ref=ring_out, dst_ref=ring_in.at[src], send_sem=sb.at[z], recv_sem=rb.at[src],
            device_id=dev, device_id_type=MESH)

    def hop_c(q, dev, piece):
        return pltpu.make_async_remote_copy(
            src_ref=total_in.at[piece], dst_ref=total_in.at[piece], send_sem=sc.at[q], recv_sem=rc.at[piece],
            device_id=dev, device_id_type=MESH)

    def phase(hop, peer_of, size, mine):
        for t in range(1, size):
            k, dev = peer_of(t)
            hop(k, dev, mine).start()

    def arrive(hop, peer_of, size):
        for t in range(1, size):
            k, dev = peer_of(size - t)
            hop(k, dev, k).wait_recv()

    phase(hop_a, struct_peer, ns, st)
    piece_in[st] = piece_out[st]
    arrive(hop_a, struct_peer, ns)
    col_out[...] = jnp.sum(piece_in[...], axis=0)
    phase(hop_y, y_peer, ny, my_y)
    col_in[my_y] = col_out[...]
    arrive(hop_y, y_peer, ny)
    ring_out[...] = jnp.sum(col_in[...], axis=0)
    phase(hop_b, z_peer, nz, my_z)
    ring_in[my_z] = ring_out[...]
    arrive(hop_b, z_peer, nz)
    total_in[st] = jnp.sum(ring_in[...], axis=0)
    phase(hop_c, struct_peer, ns, st)
    arrive(hop_c, struct_peer, ns)
    whole = jnp.concatenate([total_in[p] for p in range(ns)], axis=0)
    amp_t = whole / (stiff_ref[...] * nodes_scale)
    amp_ref[...] = amp_t
    amp = jnp.transpose(jnp.concatenate([amp_t, amp_t], axis=0))
    both = amp.astype(BF16)
    low = iota(amp.shape, 1) < 64
    left = jnp.where(low, amp, 0.0).astype(BF16)
    right = jnp.where(low, 0.0, amp).astype(BF16)

    def expand(g, _):
        at = pl.ds(pl.multiple_of(g * 256, 256), 256)
        d01 = (mm(mode_v[0, at, :], left) + mm(mode_v[1, at, :], right)).astype(BF16)
        for u in range(4):
            b = g * 4 + u
            peer = cfd_peer(b)
            send3[peer] = d01[64 * u : 64 * u + 64]

            @pl.when(b > 0)
            def _():
                hop3(peer, me).start()

        return 0

    def expand_tail(g, _):
        at = pl.ds(pl.multiple_of(g * 256, 256), 256)
        d2 = mm(mode_v[2, at, :], both)
        keep = iota((32, 128), 1) < 64
        for u in range(4):
            b = g * 4 + u
            peer = cfd_peer(b)
            send3t[peer] = jnp.where(keep, d2[64 * u : 64 * u + 32], d2[64 * u + 32 : 64 * u + 64]).astype(BF16)

            @pl.when(b > 0)
            def _():
                hop3t(peer, me).start()

        return 0

    lax.fori_loop(0, n // 4, expand, 0)
    lax.fori_loop(0, n // 4, expand_tail, 0)
    recv3[me] = send3[me]
    recv3t[me] = send3t[me]

    def choose(src, _):
        keys = column(keys_in[src].astype(F32)).astype(I32)
        low_hit = (keys & 127 == iota((128, 128), 1)).astype(F32).astype(BF16)
        high = (keys >> 7).astype(F32).astype(BF16)
        for q in range(disp.shape[0] // 128):
            picks[src, :, 128 * q : 128 * q + 128] = jnp.where(high == q, low_hit, jnp.zeros_like(low_hit))
        return 0

    lax.fori_loop(0, n, choose, 0)

    def unpack3(t, _):
        src = lax.rem(me + n - t, n)

        @pl.when(t > 0)
        def _():
            hop3(src, src).wait_recv()

        disp[pl.ds(pl.multiple_of(src * 64, 64), 64), 0:128] = recv3[src]
        return 0

    def unpack3_tail(t, _):
        src = lax.rem(me + n - t, n)

        @pl.when(t > 0)
        def _():
            hop3t(src, src).wait_recv()

        at = pl.multiple_of(src * 64, 64)
        tail = recv3t[src].astype(F32)
        other = pltpu.roll(tail, 64, 1)
        keep = iota((32, 128), 1) < 64
        disp[pl.ds(at, 32), 128:256] = jnp.where(keep, tail, other).astype(BF16)
        disp[pl.ds(at + 32, 32), 128:256] = jnp.where(keep, other, tail).astype(BF16)
        return 0

    def gather(g, _):
        sources = [cfd_peer(g * 8 + u) for u in range(8)]
        y4 = mm(jnp.concatenate([picks[src] for src in sources], axis=0), disp[:, 0:128])
        for u, src in enumerate(sources):
            send4[src] = y4[128 * u : 128 * u + CLASS_CAP].astype(BF16)

            @pl.when(g * 8 + u > 0)
            def _():
                hop4(src, me).start()

        return 0

    def gather_tail(g, _):
        sources = [cfd_peer(g * 8 + u) for u in range(8)]
        y4 = mm(jnp.concatenate([picks[src] for src in sources], axis=0), disp[:, 128:256])
        keep = iota((64, 128), 1) < 64
        for u, src in enumerate(sources):
            y = y4[128 * u : 128 * u + 128]
            send4t[src] = jnp.where(keep, y[0:64], y[64:128]).astype(BF16)

            @pl.when(g * 8 + u > 0)
            def _():
                hop4t(src, me).start()

        return 0

    lax.fori_loop(0, n, unpack3, 0)
    lax.fori_loop(0, n // 8, gather, 0)
    recv4[me] = send4[me]
    lax.fori_loop(0, n, unpack3_tail, 0)
    lax.fori_loop(0, n // 8, gather_tail, 0)
    recv4t[me] = send4t[me]

    acc_t[...] = jnp.zeros_like(acc_t)

    def place(g, hop, part, first_row):
        parts, firsts = [], []
        for u in range(4):
            t = g * 4 + u
            src = lax.rem(me + n - t, n)

            @pl.when(t > 0)
            def _():
                hop(src, src).wait_recv()

            firsts.append(src)
            parts.append(part(src))
        parts = jnp.concatenate(parts, axis=0)
        parts = jnp.transpose(parts.astype(F32)).astype(BF16)
        for b in range(count // 512):
            at = slice(512 * b, 512 * b + 512)
            classes = slot_ref[:, at] >> 7
            base = base_ref[:, at]
            pick = jnp.concatenate([base * chosen(classes, first, 128) for first in firsts], axis=0)
            acc_t[first_row : first_row + 128, at] += mm(parts, pick)
        return 0

    lax.fori_loop(0, n // 4, lambda g, _: place(g, hop4, lambda src: padded(recv4[src]), 0), 0)
    lax.fori_loop(0, n // 4, lambda g, _: place(g, hop4t, lambda src: split_halves(recv4t[src]), 128), 0)
    weight = weight_ref[...]
    out_ref[0:128, :] = (acc_t[0:128, :] * weight).astype(BF16)
    out_ref[128:192, :] = ((acc_t[128:192, :] + acc_t[192:256, :]) * weight).astype(BF16)

    def sent(t, _):
        peer = cfd_peer(t)
        for hop in (hop1, hop1t, hop1_keys, hop2, hop2t, hop3, hop3t, hop4, hop4t):
            hop(peer, me).wait_send()
        return 0

    lax.fori_loop(1, n, sent, 0)

    for t in range(1, ns):
        q, dev = struct_peer(t)
        hop_a(q, dev, st).wait_send()
        hop_c(q, dev, st).wait_send()
    for t in range(1, ny):
        y, dev = y_peer(t)
        hop_y(y, dev, my_y).wait_send()
    for t in range(1, nz):
        z, dev = z_peer(t)
        hop_b(z, dev, my_z).wait_send()


def fast(node_loads, dest_owner, dest_elem, node_weight, mode_shapes, stiffness):
    rows, width = node_loads.shape
    n, ns = lax.axis_size("cfd"), lax.axis_size("struct")
    ny = 4
    nz = n // ny
    comps, elems, modes = mode_shapes.shape
    scale = float(np.sqrt(np.float32(3.0 * rows * n * ns)))
    vmem = pl.BlockSpec(memory_space=pltpu.VMEM)
    dma = pltpu.SemaphoreType.DMA
    head, tail = (n, CLASS_CAP, 128), (n, 64, 128)
    dense, dense_tail = (n, 64, 128), (n, 32, 128)
    piece = (64 // ns, modes)
    out_t, amp_t = pl.pallas_call(
        functools.partial(fused_kernel, n, ny, ns, scale),
        out_shape=(jax.ShapeDtypeStruct((width, rows), BF16), jax.ShapeDtypeStruct((64, modes), F32)),
        in_specs=[vmem] * 5 + [pl.BlockSpec(memory_space=pl.ANY)],
        out_specs=(vmem, vmem),
        scratch_shapes=[
            pltpu.VMEM((256, rows), BF16), pltpu.VMEM((1, rows), I32), pltpu.VMEM((8, 128), F32),
            pltpu.VMEM((n, 1, 128), I32), pltpu.VMEM((n, 1, 128), I32),
            pltpu.VMEM((elems, 256), F32), pltpu.VMEM((256, rows), F32),
            *(pltpu.VMEM(v, BF16) for v in (head, head, dense, dense, dense, dense, head, head)),
            *(pltpu.VMEM(v, BF16) for v in (tail, tail, dense_tail, dense_tail, dense_tail, dense_tail, tail, tail)),
            pltpu.VMEM(mode_shapes.shape, BF16), pltpu.VMEM((64, modes), F32),
            pltpu.VMEM((ns,) + piece, F32), pltpu.VMEM((ns,) + piece, F32),
            pltpu.VMEM(piece, F32), pltpu.VMEM((ny,) + piece, F32),
            pltpu.VMEM(piece, F32), pltpu.VMEM((nz,) + piece, F32), pltpu.VMEM((ns,) + piece, F32),
            pltpu.VMEM((elems, 256), BF16), pltpu.VMEM((n, 128, elems), BF16), pltpu.VMEM((128, rows), BF16),
            *(dma((n,)) for _ in range(18)),
            dma((ns,)), dma((ns,)), dma((ny,)), dma((ny,)), dma((nz,)), dma((nz,)), dma((ns,)), dma((ns,)),
            dma(()),
        ],
        compiler_params=pltpu.CompilerParams(
            collective_id=0, has_side_effects=True, vmem_limit_bytes=56 * 1024 * 1024),
        cost_estimate=pl.CostEstimate(flops=30_000_000_000, bytes_accessed=10_000_000, transcendentals=0),
    )(
        dest_owner.reshape(1, rows), dest_elem.reshape(1, rows), node_weight.reshape(1, rows),
        node_loads.T, stiffness.reshape(1, modes), mode_shapes,
    )
    return out_t.T, amp_t.T


def per_device(*args):
    node_disp, modal_amp = fast(*args)
    crowded = jnp.isnan(modal_amp[0, 0])
    return lax.cond(crowded, lambda a, f: general(*a), lambda a, f: f, args, (node_disp, modal_amp))


def solution(mesh):
    placed = (
        P(("cfd", "struct"), None),
        P(("cfd", "struct"), None),
        P(("cfd", "struct")),
        P(("cfd", "struct")),
        P(None, ("cfd", "struct"), None),
        P(),
    )
    return jax.shard_map(
        per_device,
        mesh=mesh,
        in_specs=placed,
        out_specs=(P(("cfd", "struct"), None), P()),
        check_vma=False,
    )
```
